256 devices in a mesh: dp: 2 (over y_hi), tensor: 8 (over z), passage: 16 (over x, y_lo, core).
Axes of the slice: x: 4, y: 4 (y_hi: 2, y_lo: 2; y = y_hi * 2 + y_lo), z: 8, core: 2. Of those that a mesh axis runs over, the one named last changes fastest.
Arguments:
- answer_states: bfloat16 [2048, 4096], P(('dp', 'passage')), parts along dimension 0, may hold values from -6 to 6
- cross_keys: bfloat16 [32768, 4096], P(('dp', 'passage'), 'tensor'), parts along dimension 0, may hold values from -40 to 40
- cross_values: bfloat16 [32768, 4096], P(('dp', 'passage'), 'tensor'), parts along dimension 0, may hold values from -6 to 6
- passage_lengths: int32 [128], P(('dp', 'passage')), parts along dimension 0, may hold values from 32 to 256, as said below
- passage_sources: int32 [128], P(('dp', 'passage')), parts along dimension 0, may hold values from 0 to 31
- source_bias: float32 [32, 64], P(None, 'tensor'), may hold values from -4 to 4
- query_weight: bfloat16 [4096, 4096], P(None, 'tensor'), may hold values from -0.09375 to 0.09375
- output_weight: bfloat16 [4096, 4096], P('tensor'), may hold values from -0.09375 to 0.09375
- attn_gain: float32 [4096], replicated, may hold values from 0.5 to 1.5
- ffn_gain: float32 [4096], replicated, may hold values from 0.5 to 1.5
- gate_weight: bfloat16 [4096, 10240], P(None, ('tensor', 'passage')), may hold values from -0.09375 to 0.09375
- up_weight: bfloat16 [4096, 10240], P(None, ('tensor', 'passage')), may hold values from -0.09375 to 0.09375
- down_weight: bfloat16 [10240, 4096], P(('tensor', 'passage')), may hold values from -0.0625 to 0.0625
Outputs:
- block_out: bfloat16 [2048, 4096], P(('dp', 'passage'), 'tensor'), parts along dimension 0
The draws below stay inside these ranges and needn't reach their ends.
There are 2 independent parts, one for each index of `dp`. The reference program is written for one: setup_inputs(seed, part) draws one part's arguments, and reference() takes and returns one part's arrays. A program takes and returns all parts, laid end to end along the dimension named above; an argument that names none is the same for every part. Nothing has to cross between parts.
Inputs may be any that keep to these rules, and one draw needn't show every extreme that they name: Each passage's leading passage_lengths slots are its tokens and the rest is padding; some passage of every query is full.
All inputs are finite; a program needn't handle non-finite values.
Results may differ from the reference program's by a relative error of at most 0.0075.
Values may be sent and summed in bfloat16 or wider, within the bound.
A program may use at most 128 MiB of HBM per device.

```python
import jax
import jax.numpy as jnp
from jax import lax

D = 4096
HEADS = 64
HEAD_DIM = 64
FF = 10240
PLEN = 256
NB = 32
PASS_DEV = 4
PASSAGES = 64
KEYS = 16384
TOKENS = 1024
INNER = 4096
N_PASSAGE = 16


def draw_cross_keys(key, part):
    key = jax.random.fold_in(key, 11)
    first = jax.random.fold_in(key, 0)
    return (0.375 * jax.random.truncated_normal(first, -6.0, 6.0, (KEYS, INNER), jnp.float32)).astype(jnp.bfloat16)


def draw_passage_lengths(key, part):
    key = jax.random.fold_in(key, 12)
    first, second = jax.random.split(key, 2)
    drawn = jax.random.randint(first, (PASSAGES,), PLEN // 8, PLEN + 1)
    full_one = jax.random.randint(second, (), 0, PASSAGES)
    return jnp.where(jnp.arange(PASSAGES) == full_one, PLEN, drawn).astype(jnp.int32)


def touch_ends(values, stream_key, low, largest):
    shape = values.shape
    spot = [jax.random.randint(jax.random.fold_in(stream_key, axis), (), 0, shape[axis]) for axis in range(len(shape))]
    values = values.at[tuple(spot)].set(low)
    longest = shape.index(max(shape))
    spot[longest] = (spot[longest] + 1) % shape[longest]
    return values.at[tuple(spot)].set(largest)


def steps_of(stream_key, extent, cuts, smallest, high):
    def one(position, parts):
        heights = jax.random.uniform(jax.random.fold_in(jax.random.fold_in(stream_key, 6), position), (parts,), jnp.float32, smallest / len(cuts), high / len(cuts))
        return jnp.repeat(jnp.exp(heights), extent[position] // parts).reshape((-1,) + (1,) * (len(extent) - position - 1))

    level = one(*cuts[0])
    for cut in cuts[1:]:
        level = level * one(*cut)
    return level


def normal_values(own_key, extent, deviation, most, pieces=(), kind=jnp.bfloat16):
    values = jax.random.normal(own_key, extent, jnp.float32) * deviation
    if len(pieces) > 0:
        values = steps_of(own_key, extent, pieces, -0.22, 0.18) * values
    return jnp.clip(values, min=-most, max=most).astype(kind)


def setup_inputs(seed: int = 0, part: int = 0) -> dict:
    seeds = jax.random.split(jax.random.key(seed), 14)
    own_keys = jax.random.split(jax.random.fold_in(seeds[13], part), 14)
    return {
        "answer_states": normal_values(own_keys[0], (TOKENS, D), 1.0, 6.0, ((0, 16),)),
        "cross_keys": draw_cross_keys(jax.random.fold_in(jax.random.fold_in(seeds[13], part), 71), part),
        "cross_values": normal_values(own_keys[2], (KEYS, INNER), 1.0, 6.0, ((0, 16), (1, 8))),
        "passage_lengths": draw_passage_lengths(jax.random.fold_in(jax.random.fold_in(seeds[13], part), 71), part),
        "passage_sources": touch_ends(jax.random.randint(own_keys[4], (PASSAGES,), 0, NB), jax.random.fold_in(own_keys[4], 1), 0, NB - 1).astype(jnp.int32),
        "source_bias": normal_values(seeds[5], (NB, HEADS), 1.0, 4.0, ((1, 8),), jnp.float32),
        "query_weight": normal_values(seeds[6], (D, INNER), D ** -0.5, 0.09375, ((1, 8),)),
        "output_weight": normal_values(seeds[7], (INNER, D), INNER ** -0.5, 0.09375, ((0, 8),)),
        "attn_gain": jnp.clip(1.0 + 0.1 * jax.random.normal(seeds[8], (D,), jnp.float32), 0.5, 1.5),
        "ffn_gain": jnp.clip(1.0 + 0.1 * jax.random.normal(seeds[9], (D,), jnp.float32), 0.5, 1.5),
        "gate_weight": normal_values(seeds[10], (D, FF), D ** -0.5, 0.09375, ((1, 128),)),
        "up_weight": normal_values(seeds[11], (D, FF), D ** -0.5, 0.09375, ((1, 128),)),
        "down_weight": normal_values(seeds[12], (FF, D), FF ** -0.5, 0.0625, ((0, 128),)),
    }


def rms_scale(values, gain):
    return values * lax.rsqrt(lax.optimization_barrier(jnp.mean(values * values, axis=-1, keepdims=True)) + 1e-06) * gain.astype(jnp.float32)

def reference(answer_states, cross_keys, cross_values, passage_lengths, passage_sources, source_bias, query_weight, output_weight, attn_gain, ffn_gain, gate_weight, up_weight, down_weight):
    states = answer_states.astype(jnp.float32)
    normed = rms_scale(states, attn_gain).astype(jnp.bfloat16)
    query = jnp.dot(normed, query_weight, preferred_element_type=jnp.float32).astype(jnp.bfloat16)
    positions = jnp.arange(KEYS, dtype=jnp.int32)
    owner = (positions // PLEN).astype(jnp.int32)
    valid = positions % PLEN < passage_lengths[owner]
    bias_all = source_bias[passage_sources[owner]].astype(jnp.float32)
    query_heads = query.reshape(TOKENS, HEADS, HEAD_DIM).transpose(1, 0, 2)
    key_heads = cross_keys.reshape(KEYS, HEADS, HEAD_DIM).transpose(1, 0, 2)
    value_heads = cross_values.reshape(KEYS, HEADS, HEAD_DIM).transpose(1, 0, 2)

    def one_head(operands):
        query_h, key_h, value_h, bias_h = operands
        scores = jnp.dot(query_h, key_h.T, preferred_element_type=jnp.float32) + bias_h[None, :]
        scores = jnp.where(valid[None, :], scores, jnp.float32(-1e+30))
        blocked = scores.reshape(TOKENS, N_PASSAGE, PASS_DEV * PLEN)
        peaks = lax.optimization_barrier(jnp.max(blocked, axis=-1))
        weights = jnp.exp(blocked - peaks[..., None])
        sums = lax.optimization_barrier(jnp.sum(weights, axis=-1))
        rounded = lax.optimization_barrier(weights.astype(jnp.bfloat16))
        partial_out = jnp.einsum('tnk,nkd->tnd', rounded.astype(jnp.float32), value_h.reshape(N_PASSAGE, PASS_DEV * PLEN, HEAD_DIM).astype(jnp.float32))
        highest = lax.optimization_barrier(jnp.max(peaks, axis=-1))
        factor = jnp.exp(peaks - highest[:, None])
        numer = lax.optimization_barrier(jnp.sum(partial_out * factor[..., None], axis=1))
        denom = lax.optimization_barrier(jnp.sum(sums * factor, axis=1))
        return numer / denom[:, None]
    heads_out = lax.map(one_head, (query_heads, key_heads, value_heads, bias_all.T))
    attended = heads_out.transpose(1, 0, 2).reshape(TOKENS, INNER).astype(jnp.bfloat16)
    middle = states + jnp.dot(attended, output_weight, preferred_element_type=jnp.float32)
    ffn_in = rms_scale(middle, ffn_gain).astype(jnp.bfloat16)
    gate = jnp.dot(ffn_in, gate_weight, preferred_element_type=jnp.float32)
    upper = jnp.dot(ffn_in, up_weight, preferred_element_type=jnp.float32)
    hidden_units = (jax.nn.gelu(gate, approximate=True) * upper).astype(jnp.bfloat16)
    result = middle + jnp.dot(hidden_units, down_weight, preferred_element_type=jnp.float32)
    return result.astype(jnp.bfloat16)
```

```python
import functools

import jax
import jax.numpy as jnp
from jax import lax
from jax.experimental import pallas as pl
from jax.experimental.pallas import tpu as pltpu
from jax.sharding import PartitionSpec as P

PLEN = 256
EPS = 1e-06
BF = jnp.bfloat16
F32 = jnp.float32
MESH = pl.DeviceIdType.MESH
NT = (((1,), (1,)), ((), ()))


def remote(src, dst, send_sem, recv_sem, **where):
    return pltpu.make_async_remote_copy(
        src_ref=src,
        dst_ref=dst,
        send_sem=send_sem,
        recv_sem=recv_sem,
        device_id=where,
        device_id_type=MESH,
    )


def iota(shape, axis):
    return lax.broadcasted_iota(jnp.int32, shape, axis)


def block_kernel(
    states_h, keys_h, values_h, lens_s, srcs_s, bias_s, wq_h, wo_h, again, fgain, gate_h, up_h, down_h,
    out_ref,
    states, wq, wo, kaug, vaug, qaug, sel, expand,
    qall, ostage, srecv, rsend, rrecv,
    wsend, wrecv, wown, mid, midr, fbuf, acc, oown, osend, orecv, fown, fsend, frecv, wall,
    load_sem, wq_sem, ws, wr, qs, qr, qfs, qfr, ss, sr, rs, rr, as_, ar, ms, mr,
    zs, zr, xs, xr, os_, or_, fs, fr,
):
    dp = lax.axis_index("dp")
    z = lax.axis_index("tensor")
    p = lax.axis_index("passage")
    x = p // 4
    yl = (p // 2) % 2
    c = p % 2
    chip = p // 2
    sib = p + 1 - 2 * c
    zpar = z % 2
    zcol = z // 2
    zmate = z + 1 - 2 * zpar

    def peer(dx, dy):
        return ((x + dx) % 4) * 4 + ((yl + dy) % 2) * 2 + c

    def offsets(i):
        d = i // 2
        return d + d // 2 - 2 * (d // 3), i % 2

    def taker(i):
        dx, dy = offsets(i)
        return peer(dx, dy)

    def giver(i):
        dx, dy = offsets(i)
        return peer(4 - dx, 2 - dy)

    ydev = dict(dp=(dp + c) % 2, passage=peer(0, 1))
    zdev = dict(tensor=(z + 1 - 2 * c + 8) % 8)

    barrier = pltpu.get_barrier_semaphore()
    for i in range(1, 8):
        pl.semaphore_signal(barrier, inc=1, device_id={"passage": taker(i)}, device_id_type=MESH)
        pl.semaphore_signal(barrier, inc=1, device_id={"tensor": (z + i) % 8}, device_id_type=MESH)
    pl.semaphore_signal(barrier, inc=1, device_id={"passage": sib}, device_id_type=MESH)
    pl.semaphore_signal(barrier, inc=1, device_id=ydev, device_id_type=MESH)

    loads = [pltpu.make_async_copy(states_h, states, load_sem.at[0])]
    loads[0].start()
    wq_loads = []
    for k in range(4):
        rows = pl.ds(1024 * k, 1024)
        wq_loads.append(pltpu.make_async_copy(wq_h.at[rows], wq.at[rows], wq_sem.at[k]))
        wq_loads[k].start()
    kv_loads = []
    for j in range(4):
        lanes = pl.ds(128 * j, 128)
        kv_loads.append(pltpu.make_async_copy(keys_h.at[:, lanes], kaug.at[j, :, pl.ds(0, 128)], load_sem.at[2 + j]))
        kv_loads.append(pltpu.make_async_copy(values_h.at[:, lanes], vaug.at[j, :, pl.ds(0, 128)], load_sem.at[6 + j]))
    for copy in kv_loads:
        copy.start()
    wo_load = pltpu.make_async_copy(wo_h, wo, load_sem.at[1])
    wo_load.start()
    own_loads = []
    for m, ref in enumerate((gate_h, up_h, down_h)):
        own_loads.append(pltpu.make_async_copy(ref, wall.at[m, 0], load_sem.at[10 + m]))
        own_loads[m].start()

    loads[0].wait()
    square = jnp.zeros((64, 1), F32)
    for k in range(4):
        part = states[:, 1024 * k : 1024 * (k + 1)].astype(F32)
        square = square + jnp.sum(part * part, axis=-1, keepdims=True)
    scale = lax.rsqrt(square * (1.0 / 4096) + EPS)
    query = jnp.zeros((64, 512), F32)
    for k in range(4):
        cols = slice(1024 * k, 1024 * (k + 1))
        normed = (states[:, cols].astype(F32) * scale * again[:, cols]).astype(BF)
        wq_loads[k].wait()
        query = query + jnp.dot(normed, wq[cols, :], preferred_element_type=F32)
    qall[p] = query.astype(BF)

    pl.semaphore_wait(barrier, 16)

    def q_send(i):
        return remote(qall.at[p], qall.at[p], qs.at[i], qr.at[i], passage=taker(i))

    def q_arrival(i):
        slot = qall.at[giver(i)]
        return remote(slot, slot, qs.at[i], qr.at[i], passage=taker(i))

    def q_hand(i):
        slot = qall.at[giver(i)]
        return remote(slot, slot, qfs.at[i], qfr.at[i], passage=sib)

    def q_handed(i):
        dx, dy = offsets(i)
        slot = qall.at[((x + 4 - dx) % 4) * 4 + ((yl + 2 - dy) % 2) * 2 + 1 - c]
        return remote(slot, slot, qfs.at[i], qfr.at[i], passage=sib)

    q_hand(0).start()
    for i in range(1, 8):
        q_send(i).start()

    def w_copy(kind, m):
        own = (gate_h, up_h, down_h)[m]
        if kind == 0:
            src, slot, dev = own, 1, ydev
        elif kind == 1:
            src, slot, dev = own, 2, zdev
        elif kind == 2:
            src, slot, dev = own, 4, dict(passage=sib)
        elif kind < 6:
            src, slot, dev = wall.at[m, kind - 2], kind + 2, dict(passage=sib)
        else:
            src, slot, dev = wall.at[m, 2], 3, ydev
        return remote(src, wall.at[m, slot], ws.at[kind, m], wr.at[kind, m], **dev)

    for m in range(3):
        for kind in range(3):
            w_copy(kind, m).start()

    lane = iota((256, 128), 1)
    row = iota((256, 128), 0)
    for j in range(4):
        for pp in range(4):
            table = jnp.where(lane == 0, jnp.where(row >= lens_s[pp], F32(-1e30), F32(0)), F32(0))
            for e in range(2):
                value = jnp.full((256, 128), bias_s[2 * j + e, srcs_s[pp]], F32)
                high = value.astype(BF).astype(F32)
                middle = (value - high).astype(BF).astype(F32)
                low = value - high - middle
                first = 1 + 3 * e
                table = jnp.where(lane == first, high, table)
                table = jnp.where(lane == first + 1, middle, table)
                table = jnp.where(lane == first + 2, low, table)
            kaug[j, 256 * pp : 256 * (pp + 1), 128:256] = table.astype(BF)
        vaug[j, :, 128:256] = jnp.ones((1024, 128), BF)
    upper = row < 128
    qaug[...] = jnp.where(
        (lane == 0) | (upper & (lane >= 1) & (lane < 4)) | (~upper & (lane >= 4) & (lane < 7)), F32(1), F32(0)
    ).astype(BF)
    srow, scol = iota((1536, 128), 0), iota((1536, 128), 1)
    sel[...] = jnp.where((srow % 64 == 0) & (scol == srow // 64), F32(1), F32(0)).astype(BF)
    erow, ecol = iota((128, 512), 0), iota((128, 512), 1)
    expand[...] = jnp.where((erow < 24) & (erow % 8 == ecol // 64), F32(1), F32(0)).astype(BF)
    for copy in kv_loads:
        copy.wait()

    def attend(i):
        dx, dy = offsets(i)
        source = ((x + 4 - dx) % 4) * 2 + (yl + 2 - dy) % 2
        rows = qall[pl.ds(2 * source, 2)].reshape(128, 512)
        head_lane = iota((128, 128), 1) < 64
        zero = jnp.zeros((128, 128), BF)
        for j in range(4):
            cols = slice(128 * j, 128 * (j + 1))
            pair = rows[:, cols]
            both = jnp.concatenate([jnp.where(head_lane, pair, zero), jnp.where(head_lane, zero, pair)], axis=0)
            both = jnp.concatenate([both, qaug[...]], axis=1)
            scores = lax.dot_general(both, kaug[j], NT, preferred_element_type=F32)
            peak = jnp.max(scores, axis=1, keepdims=True)
            weights = jnp.exp(scores - peak).astype(BF)
            result = jnp.dot(weights, vaug[j], preferred_element_type=F32)
            total = result[:, 128:]
            part = result[:, :128] / total
            level = peak + jnp.log(total)
            part = jnp.where(head_lane, part[:128], part[128:])
            level = jnp.where(head_lane, level[:128], level[128:])
            ostage[i, 0, 0, :, cols] = part[:64]
            ostage[i, 1, 0, :, cols] = part[64:]
            ostage[i, 0, 1, :, cols] = level[:64]
            ostage[i, 1, 1, :, cols] = level[64:]

    def half_send(i):
        return remote(ostage.at[i, 1 - c], srecv.at[i], ss.at[i], sr.at[i], passage=sib)

    def part_send(i):
        return remote(rsend.at[i], rrecv.at[i], rs.at[i], rr.at[i], passage=giver(i))

    def merge(i):
        half_send(i).wait_recv()
        part_a, level_a = ostage[i, c, 0], ostage[i, c, 1]
        part_b, level_b = srecv[i, 0], srecv[i, 1]
        highest = jnp.maximum(level_a, level_b)
        weight_a = jnp.exp(level_a - highest)
        weight_b = jnp.exp(level_b - highest)
        total = weight_a + weight_b
        rsend[i, :, 0:512] = ((weight_a * part_a + weight_b * part_b) / total).astype(BF)
        level = highest + jnp.log(total)
        high = level.astype(BF)
        rest = level - high.astype(F32)
        middle = rest.astype(BF)
        low = (rest - middle.astype(F32)).astype(BF)
        pieces = jnp.concatenate([high, middle, low], axis=1)
        rsend[i, :, 512:640] = jnp.dot(pieces, sel[...], preferred_element_type=F32).astype(BF)

    def turn(i, carry):
        @pl.when(i < 7)
        def _():
            q_arrival(i + 1).wait_recv()
            q_hand(i + 1).start()

        q_handed(i).wait_recv()
        attend(i)
        half_send(i).start()

        @pl.when(i >= 1)
        def _():
            merge(i - 1)

        @pl.when(i >= 2)
        def _():
            part_send(i - 1).start()

        return carry

    lax.fori_loop(0, 8, turn, 0)
    merge(7)
    part_send(7).start()

    for m in range(3):
        w_copy(1, m).wait_recv()
        w_copy(6, m).start()
        w_copy(4, m).start()
    for m in range(3):
        w_copy(0, m).wait_recv()
        w_copy(3, m).start()

    for i in range(1, 8):
        part_send(i).wait_recv()
    levels = [
        jnp.dot((rsend[0] if i == 0 else rrecv[i])[:, 512:640], expand[...], preferred_element_type=F32)
        for i in range(8)
    ]
    highest = functools.reduce(jnp.maximum, levels)
    total = jnp.zeros((64, 512), F32)
    joined = jnp.zeros((64, 512), F32)
    for i in range(8):
        weight = jnp.exp(levels[i] - highest)
        total = total + weight
        joined = joined + weight * (rsend[0] if i == 0 else rrecv[i])[:, 0:512].astype(F32)
    attended = (joined / total).astype(BF)

    wo_load.wait()

    def wo_send(o):
        to = (z + o) % 8
        return remote(wsend.at[to // 2, to % 2], wrecv.at[o], as_.at[o], ar.at[o], tensor=to)

    for k in (2, 1, 3, 0):
        block = (zcol + k) % 4
        lanes = pl.ds(pl.multiple_of(block * 1024, 1024), 1024)
        product = jnp.dot(attended, wo[:, lanes], preferred_element_type=F32)
        wsend[block, 0] = product[:32].astype(BF)
        wsend[block, 1] = product[32:].astype(BF)
        if k == 0:
            wown[0] = product[:32]
            wown[1] = product[32:]
            wo_send((zmate - z + 8) % 8).start()
        else:
            for e in range(2):
                wo_send((2 * block + e - z + 8) % 8).start()

    lanes = pl.ds(pl.multiple_of(zcol * 1024, 1024), 1024)
    middle = states[pl.ds(pl.multiple_of(zpar * 32, 32), 32), lanes].astype(F32) + wown[zpar]
    for o in range(1, 8):
        wo_send(o).wait_recv()
        middle = middle + wrecv[o].astype(F32)
    mid[0] = middle[:, :512]
    mid[1] = middle[:, 512:]
    fbuf[zcol, x] = (middle * fgain[:, lanes]).astype(BF)

    def z_send(o):
        slot = fbuf.at[zcol, x]
        return remote(slot, slot, zs.at[o], zr.at[o], tensor=(z + 2 * o) % 8)

    def z_arrival(o):
        slot = fbuf.at[((z + 8 - 2 * o) % 8) // 2, x]
        return remote(slot, slot, zs.at[o], zr.at[o], tensor=(z + 2 * o) % 8)

    def x_send(o, d):
        slot = fbuf.at[((z + 8 - 2 * o) % 8) // 2, x]
        return remote(slot, slot, xs.at[o, d], xr.at[o, d], passage=peer(d, 0))

    def x_arrival(o, d):
        slot = fbuf.at[((z + 8 - 2 * o) % 8) // 2, (x + 4 - d) % 4]
        return remote(slot, slot, xs.at[o, d], xr.at[o, d], passage=peer(d, 0))

    for o in (1, 3, 2):
        z_send(o).start()
    for d in (1, 3, 2):
        x_send(0, d).start()
    mid_send = remote(mid.at[1 - zpar], midr, ms, mr, tensor=zmate)
    mid_send.start()

    for m in range(3):
        w_copy(6, m).wait_recv()
        w_copy(5, m).start()
    for copy in own_loads:
        copy.wait()
    for kind in (2, 3, 4, 5):
        for m in range(2):
            w_copy(kind, m).wait_recv()

    squares = jnp.zeros((128, 1), F32)
    order = (0, 1, 3, 2)
    for n, o in enumerate(order):
        if n < 3:
            z_arrival(order[n + 1]).wait_recv()
            for d in (1, 3, 2):
                x_send(order[n + 1], d).start()
        for d in (1, 3, 2):
            x_arrival(o, d).wait_recv()
        block = ((z + 8 - 2 * o) % 8) // 2
        lanes = pl.ds(pl.multiple_of(block * 1024, 1024), 1024)
        piece = fbuf[block].reshape(128, 1024)
        plain = piece.astype(F32) / fgain[:, lanes]
        squares = squares + jnp.sum(plain * plain, axis=-1, keepdims=True)
        for m in range(2):
            weight = wall[m, :, :, lanes].reshape(640, 1024)
            product = lax.dot_general(piece, weight, NT, preferred_element_type=F32)
            if n == 0:
                acc[m] = product
            else:
                acc[m] += product
    scale = lax.rsqrt(squares * (1.0 / 4096) + EPS)
    gate = acc[0] * scale
    hidden = (jax.nn.gelu(gate, approximate=True) * (acc[1] * scale)).astype(BF)

    for kind in (2, 3, 4, 5):
        w_copy(kind, 2).wait_recv()

    def o_send(block, k, d):
        return remote(osend.at[block, (x + d) % 4], orecv.at[k, d], os_.at[k, d], or_.at[k, d], passage=peer(d, 0))

    for k in (2, 1, 3, 0):
        block = (zcol + k) % 4
        lanes = pl.ds(pl.multiple_of(block * 1024, 1024), 1024)
        product = jnp.dot(hidden, wall[2, :, :, lanes].reshape(640, 1024), preferred_element_type=F32)
        product = product.reshape(4, 32, 1024)
        osend[block] = product.astype(BF)
        oown[k] = product
        for d in (1, 3, 2):
            o_send(block, k, d).start()

    def f_send(o):
        to = (z + o) % 8
        return remote(fsend.at[to // 2, to % 2], frecv.at[o], fs.at[o], fr.at[o], tensor=to)

    for k in (2, 1, 3, 0):
        block = (zcol + k) % 4
        total = oown[k, x]
        for d in (1, 3, 2):
            o_send(block, k, d).wait_recv()
            total = total + orecv[k, d].astype(F32)
        fsend[block, 0] = total[:, :512].astype(BF)
        fsend[block, 1] = total[:, 512:].astype(BF)
        if k == 0:
            fown[0] = total[:, :512]
            fown[1] = total[:, 512:]
            f_send((zmate - z + 8) % 8).start()
        else:
            for e in range(2):
                f_send((2 * block + e - z + 8) % 8).start()

    mid_send.wait_recv()
    mine = mid[zpar] + fown[zpar]
    other = midr[...]
    for o in range(1, 8):
        f_send(o).wait_recv()
        if o % 2 == 0:
            mine = mine + frecv[o].astype(F32)
        else:
            other = other + frecv[o].astype(F32)
    out_ref[pl.ds(pl.multiple_of(zpar * 32, 32), 32), :] = mine.astype(BF)
    out_ref[pl.ds(pl.multiple_of(32 - zpar * 32, 32), 32), :] = other.astype(BF)

    for i in range(8):
        q_hand(i).wait_send()
        half_send(i).wait_send()
        if i > 0:
            q_send(i).wait_send()
            part_send(i).wait_send()
            wo_send(i).wait_send()
            f_send(i).wait_send()
    for m in range(3):
        for kind in range(7):
            w_copy(kind, m).wait_send()
    mid_send.wait_send()
    for o in range(4):
        if o > 0:
            z_send(o).wait_send()
        for d in (1, 2, 3):
            x_send(o, d).wait_send()
            o_send((zcol + o) % 4, o, d).wait_send()


def on_device(
    answer_states, cross_keys, cross_values, passage_lengths, passage_sources, source_bias,
    query_weight, output_weight, attn_gain, ffn_gain, gate_weight, up_weight, down_weight,
):
    hbm = pl.BlockSpec(memory_space=pl.ANY)
    smem = pl.BlockSpec(memory_space=pltpu.SMEM)
    vmem = pl.BlockSpec(memory_space=pltpu.VMEM)
    dma = pltpu.SemaphoreType.DMA
    return pl.pallas_call(
        block_kernel,
        out_shape=jax.ShapeDtypeStruct((64, 512), BF),
        in_specs=[hbm, hbm, hbm, smem, smem, smem, hbm, hbm, vmem, vmem, hbm, hbm, hbm],
        out_specs=vmem,
        scratch_shapes=[
            pltpu.VMEM((64, 4096), BF),
            pltpu.VMEM((4096, 512), BF),
            pltpu.VMEM((512, 4096), BF),
            pltpu.VMEM((4, 1024, 256), BF),
            pltpu.VMEM((4, 1024, 256), BF),
            pltpu.VMEM((256, 128), BF),
            pltpu.VMEM((1536, 128), BF),
            pltpu.VMEM((128, 512), BF),
            pltpu.VMEM((16, 64, 512), BF),
            pltpu.VMEM((8, 2, 2, 64, 512), F32),
            pltpu.VMEM((8, 2, 64, 512), F32),
            pltpu.VMEM((8, 64, 640), BF),
            pltpu.VMEM((8, 64, 640), BF),
            pltpu.VMEM((4, 2, 32, 1024), BF),
            pltpu.VMEM((8, 32, 1024), BF),
            pltpu.VMEM((2, 32, 1024), F32),
            pltpu.VMEM((2, 32, 512), F32),
            pltpu.VMEM((32, 512), F32),
            pltpu.VMEM((4, 4, 32, 1024), BF),
            pltpu.VMEM((2, 128, 640), F32),
            pltpu.VMEM((4, 4, 32, 1024), F32),
            pltpu.VMEM((4, 4, 32, 1024), BF),
            pltpu.VMEM((4, 4, 32, 1024), BF),
            pltpu.VMEM((2, 32, 512), F32),
            pltpu.VMEM((4, 2, 32, 512), BF),
            pltpu.VMEM((8, 32, 512), BF),
            pltpu.VMEM((3, 8, 80, 4096), BF),
            dma((13,)), dma((4,)),
            dma((7, 3)), dma((7, 3)),
            dma((8,)), dma((8,)), dma((8,)), dma((8,)),
            dma((8,)), dma((8,)), dma((8,)), dma((8,)),
            dma((8,)), dma((8,)), dma, dma,
            dma((4,)), dma((4,)), dma((4, 4)), dma((4, 4)),
            dma((4, 4)), dma((4, 4)), dma((8,)), dma((8,)),
        ],
        compiler_params=pltpu.CompilerParams(
            collective_id=0, has_side_effects=True, vmem_limit_bytes=60 * 1024 * 1024
        ),
        cost_estimate=pl.CostEstimate(flops=5_000_000_000, bytes_accessed=14_000_000, transcendentals=9_000_000),
        name="decoder_block",
    )(
        answer_states, cross_keys, cross_values, passage_lengths, passage_sources, source_bias.T,
        query_weight, output_weight, attn_gain.reshape(1, 4096), ffn_gain.reshape(1, 4096),
        gate_weight.T, up_weight.T, down_weight,
    )


def solution(mesh):
    return jax.shard_map(
        on_device,
        mesh=mesh,
        in_specs=(
            P(("dp", "passage"), None),
            P(("dp", "passage"), "tensor"),
            P(("dp", "passage"), "tensor"),
            P(("dp", "passage")),
            P(("dp", "passage")),
            P(None, "tensor"),
            P(None, "tensor"),
            P("tensor", None),
            P(),
            P(),
            P(None, ("tensor", "passage")),
            P(None, ("tensor", "passage")),
            P(("tensor", "passage"), None),
        ),
        out_specs=P(("dp", "passage"), "tensor"),
        check_vma=False,
    )
```

```python
import functools

import jax
import jax.numpy as jnp
from jax import lax
from jax.experimental import pallas as pl
from jax.experimental.pallas import tpu as pltpu
from jax.sharding import PartitionSpec as P

PLEN = 256
EPS = 1e-06
BF = jnp.bfloat16
F32 = jnp.float32
MESH = pl.DeviceIdType.MESH
NT = (((1,), (1,)), ((), ()))


def remote(src, dst, send_sem, recv_sem, **where):
    return pltpu.make_async_remote_copy(
        src_ref=src,
        dst_ref=dst,
        send_sem=send_sem,
        recv_sem=recv_sem,
        device_id=where,
        device_id_type=MESH,
    )


def iota(shape, axis):
    return lax.broadcasted_iota(jnp.int32, shape, axis)


def block_kernel(
    states_h, keys_h, values_h, lens_s, srcs_s, bias_s, wq_h, wo_h, again, fgain, gate_h, up_h, down_h,
    out_ref,
    states, wq, wo, kaug, vaug, qaug, sel, expand,
    qall, ostage, srecv, rsend, rrecv,
    wsend, wrecv, wown, mid, midr, fbuf, acc, oown, osend, orecv, fown, fsend, frecv, wall,
    load_sem, wq_sem, ws, wr, qs, qr, qfs, qfr, ss, sr, rs, rr, as_, ar, ms, mr,
    zs, zr, xs, xr, os_, or_, fs, fr,
):
    dp = lax.axis_index("dp")
    z = lax.axis_index("tensor")
    p = lax.axis_index("passage")
    x = p // 4
    yl = (p // 2) % 2
    c = p % 2
    sib = p + 1 - 2 * c
    zpar = z % 2
    zcol = z // 2
    zmate = z + 1 - 2 * zpar

    def peer(dx, dy):
        return ((x + dx) % 4) * 4 + ((yl + dy) % 2) * 2 + c

    def shift(t):
        return t + t // 2 - 2 * (t // 3)

    ydev = dict(dp=(dp + c) % 2, passage=peer(0, 1))
    yfar = dict(dp=1 - dp, passage=peer(0, 1))
    zdev = dict(tensor=(z + 1 - 2 * c + 8) % 8)

    barrier = pltpu.get_barrier_semaphore()
    for i in range(1, 8):
        pl.semaphore_signal(barrier, inc=1, device_id={"passage": peer(i // 2, i % 2)}, device_id_type=MESH)
        pl.semaphore_signal(barrier, inc=1, device_id={"tensor": (z + i) % 8}, device_id_type=MESH)
    pl.semaphore_signal(barrier, inc=1, device_id={"passage": sib}, device_id_type=MESH)
    pl.semaphore_signal(barrier, inc=1, device_id=yfar, device_id_type=MESH)

    states_load = pltpu.make_async_copy(states_h, states, load_sem.at[0])
    states_load.start()
    wq_loads = []
    for k in range(4):
        rows = pl.ds(1024 * k, 1024)
        wq_loads.append(pltpu.make_async_copy(wq_h.at[rows], wq.at[rows], wq_sem.at[k]))
        wq_loads[k].start()
    kv_loads = []
    for j in range(4):
        lanes = pl.ds(128 * j, 128)
        kv_loads.append(pltpu.make_async_copy(keys_h.at[:, lanes], kaug.at[j, :, pl.ds(0, 128)], load_sem.at[2 + j]))
        kv_loads.append(pltpu.make_async_copy(values_h.at[:, lanes], vaug.at[j, :, pl.ds(0, 128)], load_sem.at[6 + j]))
    wo_load = pltpu.make_async_copy(wo_h, wo, load_sem.at[1])
    own_loads = [
        pltpu.make_async_copy(ref, wall.at[m, 0], load_sem.at[10 + m]) for m, ref in enumerate((gate_h, up_h, down_h))
    ]

    states_load.wait()
    square = jnp.zeros((64, 1), F32)
    for k in range(4):
        part = states[:, 1024 * k : 1024 * (k + 1)].astype(F32)
        square = square + jnp.sum(part * part, axis=-1, keepdims=True)
    scale = lax.rsqrt(square * (1.0 / 4096) + EPS)
    query = jnp.zeros((64, 512), F32)
    for k in range(4):
        cols = slice(1024 * k, 1024 * (k + 1))
        normed = (states[:, cols].astype(F32) * scale * again[:, cols]).astype(BF)
        wq_loads[k].wait()
        query = query + jnp.dot(normed, wq[cols, :], preferred_element_type=F32)
    for copy in kv_loads:
        copy.start()
    qall[0, x, c, yl] = query[:32].astype(BF)
    qall[1, x, c, yl] = query[32:].astype(BF)

    pl.semaphore_wait(barrier, 16)

    def q_send(b, t, dy):
        slot = qall.at[b, x, c, yl]
        return remote(slot, slot, qs.at[b, t, dy], qr.at[b, t, dy], passage=peer(shift(t), dy))

    def q_arrival(b, t, dy):
        slot = qall.at[b, (x + 4 - shift(t)) % 4, c, (yl + dy) % 2]
        return remote(slot, slot, qs.at[b, t, dy], qr.at[b, t, dy], passage=peer(shift(t), dy))

    def q_hand(b, t):
        slab = qall.at[b, (x + 4 - shift(t)) % 4, c]
        return remote(slab, slab, qfs.at[b, t], qfr.at[b, t], passage=sib)

    def q_handed(b, t):
        slab = qall.at[b, (x + 4 - shift(t)) % 4, 1 - c]
        return remote(slab, slab, qfs.at[b, t], qfr.at[b, t], passage=sib)

    others = [(t, dy) for t in range(4) for dy in range(2) if (t, dy) != (0, 0)]
    for t, dy in others:
        q_send(0, t, dy).start()

    def w_copy(kind, m):
        own = (gate_h, up_h, down_h)[m]
        if kind == 0:
            src, slot, dev = own, 2, yfar if m == 2 else ydev
        elif kind == 1:
            src, slot, dev = own, 4, zdev
        elif kind == 2:
            src, slot, dev = own, 1, dict(passage=sib)
        elif kind < 6:
            src, slot, dev = wall.at[m, 2 * kind - 4], 2 * kind - 3, dict(passage=sib)
        else:
            src, slot, dev = wall.at[m, 4], 6, ydev
        return remote(src, wall.at[m, slot], ws.at[kind, m], wr.at[kind, m], **dev)

    w_copy(0, 0).start()
    for m in range(3):
        w_copy(1, m).start()

    lane = iota((256, 128), 1)
    row = iota((256, 128), 0)
    for j in range(4):
        for pp in range(4):
            table = jnp.where(lane == 0, jnp.where(row >= lens_s[pp], F32(-1e30), F32(0)), F32(0))
            for e in range(2):
                value = jnp.full((256, 128), bias_s[2 * j + e, srcs_s[pp]], F32)
                high = value.astype(BF).astype(F32)
                middle = (value - high).astype(BF).astype(F32)
                low = value - high - middle
                first = 1 + 3 * e
                table = jnp.where(lane == first, high, table)
                table = jnp.where(lane == first + 1, middle, table)
                table = jnp.where(lane == first + 2, low, table)
            kaug[j, 256 * pp : 256 * (pp + 1), 128:256] = table.astype(BF)
        vaug[j, :, 128:256] = jnp.ones((1024, 128), BF)
    upper = row < 128
    qaug[...] = jnp.where(
        (lane == 0) | (upper & (lane >= 1) & (lane < 4)) | (~upper & (lane >= 4) & (lane < 7)), F32(1), F32(0)
    ).astype(BF)
    srow, scol = iota((1536, 128), 0), iota((1536, 128), 1)
    sel[...] = jnp.where((srow % 64 == 0) & (scol == srow // 64), F32(1), F32(0)).astype(BF)
    erow, ecol = iota((128, 512), 0), iota((128, 512), 1)
    expand[...] = jnp.where((erow < 24) & (erow % 8 == ecol // 64), F32(1), F32(0)).astype(BF)
    q_arrival(0, 0, 1).wait_recv()
    q_hand(0, 0).start()
    for copy in kv_loads:
        copy.wait()
    wo_load.start()
    for copy in own_loads:
        copy.start()
    for m in range(3):
        w_copy(2, m).start()

    def attend(n):
        rows = qall[n // 4, (x + 4 - shift(n % 4)) % 4].reshape(128, 512)
        head_lane = iota((128, 128), 1) < 64
        zero = jnp.zeros((128, 128), BF)
        for j in range(4):
            cols = slice(128 * j, 128 * (j + 1))
            pair = rows[:, cols]
            both = jnp.concatenate([jnp.where(head_lane, pair, zero), jnp.where(head_lane, zero, pair)], axis=0)
            both = jnp.concatenate([both, qaug[...]], axis=1)
            scores = lax.dot_general(both, kaug[j], NT, preferred_element_type=F32)
            peak = jnp.max(scores, axis=1, keepdims=True)
            weights = jnp.exp(scores - peak).astype(BF)
            result = jnp.dot(weights, vaug[j], preferred_element_type=F32)
            part = jnp.where(head_lane, result[:128, :128], result[128:, :128])
            total = jnp.where(head_lane, result[:128, 128:], result[128:, 128:])
            peak = jnp.where(head_lane, peak[:128], peak[128:])
            for e in range(2):
                half = slice(64 * e, 64 * (e + 1))
                ostage[n, e, 0, :, cols] = part[half]
                ostage[n, e, 1, :, cols] = total[half]
                ostage[n, e, 2, :, cols] = peak[half]

    def half_send(n):
        return remote(ostage.at[n, 1 - c], srecv.at[n], ss.at[n], sr.at[n], passage=sib)

    def part_send(b, t, dy):
        to = ((x + 4 - shift(t)) % 4) * 4 + ((yl + dy) % 2) * 2 + c
        return remote(
            rsend.at[4 * b + t, (yl + dy) % 2], rrecv.at[b, t, dy], rs.at[b, t, dy], rr.at[b, t, dy], passage=to
        )

    def merge(n):
        half_send(n).wait_recv()
        peak_a, peak_b = ostage[n, c, 2], srecv[n, 2]
        highest = jnp.maximum(peak_a, peak_b)
        weight_a = jnp.exp(peak_a - highest)
        weight_b = jnp.exp(peak_b - highest)
        total = weight_a * ostage[n, c, 1] + weight_b * srecv[n, 1]
        part = ((weight_a * ostage[n, c, 0] + weight_b * srecv[n, 0]) / total).astype(BF)
        level = highest + jnp.log(total)
        high = level.astype(BF)
        rest = level - high.astype(F32)
        middle = rest.astype(BF)
        low = (rest - middle.astype(F32)).astype(BF)
        pieces = jnp.concatenate([high, middle, low], axis=1)
        packed = jnp.dot(pieces, sel[...], preferred_element_type=F32).astype(BF)
        for e in range(2):
            rsend[n, e, :, 0:512] = part[32 * e : 32 * (e + 1)]
            rsend[n, e, :, 512:640] = packed[32 * e : 32 * (e + 1)]
        b, t = n // 4, n % 4
        part_send(b, t, 1).start()

        @pl.when(t > 0)
        def _():
            part_send(b, t, 0).start()

    def wo_send(b, o):
        to = (z + o) % 8
        return remote(wsend.at[b, to // 2, to % 2], wrecv.at[b, o], as_.at[b, o], ar.at[b, o], tensor=to)

    def project(b):
        for t, dy in others:
            part_send(b, t, dy).wait_recv()
        parts = [rsend[4 * b, yl]] + [rrecv[b, t, dy] for t, dy in others]
        levels = [jnp.dot(part[:, 512:640], expand[...], preferred_element_type=F32) for part in parts]
        highest = functools.reduce(jnp.maximum, levels)
        total = jnp.zeros((32, 512), F32)
        joined = jnp.zeros((32, 512), F32)
        for part, level in zip(parts, levels):
            weight = jnp.exp(level - highest)
            total = total + weight
            joined = joined + weight * part[:, 0:512].astype(F32)
        attended = (joined / total).astype(BF)
        for k in (2, 1, 3, 0):
            block = (zcol + k) % 4
            lanes = pl.ds(pl.multiple_of(block * 1024, 1024), 1024)
            product = jnp.dot(attended, wo[:, lanes], preferred_element_type=F32)
            wsend[b, block, 0] = product[:16].astype(BF)
            wsend[b, block, 1] = product[16:].astype(BF)
            if k == 0:
                wown[b, 0] = product[:16]
                wown[b, 1] = product[16:]
                wo_send(b, (zmate - z + 8) % 8).start()
            else:
                for e in range(2):
                    wo_send(b, (2 * block + e - z + 8) % 8).start()

    def z_send(b, o):
        slot = fbuf.at[zcol, b, x]
        return remote(slot, slot, zs.at[b, o], zr.at[b, o], tensor=(z + 2 * o) % 8)

    def z_arrival(b, o):
        slot = fbuf.at[((z + 8 - 2 * o) % 8) // 2, b, x]
        return remote(slot, slot, zs.at[b, o], zr.at[b, o], tensor=(z + 2 * o) % 8)

    def x_send(b, o, d):
        slot = fbuf.at[((z + 8 - 2 * o) % 8) // 2, b, x]
        return remote(slot, slot, xs.at[b, o, d], xr.at[b, o, d], passage=peer(d, 0))

    def x_arrival(b, o, d):
        slot = fbuf.at[((z + 8 - 2 * o) % 8) // 2, b, (x + 4 - d) % 4]
        return remote(slot, slot, xs.at[b, o, d], xr.at[b, o, d], passage=peer(d, 0))

    def residual(b):
        lanes = pl.ds(pl.multiple_of(zcol * 1024, 1024), 1024)
        rows = pl.ds(pl.multiple_of(32 * b + zpar * 16, 16), 16)
        middle = states[rows, lanes].astype(F32) + wown[b, zpar]
        for o in range(1, 8):
            wo_send(b, o).wait_recv()
            middle = middle + wrecv[b, o].astype(F32)
        mid[0, 16 * b : 16 * b + 16] = middle[:, :512]
        mid[1, 16 * b : 16 * b + 16] = middle[:, 512:]
        fbuf[zcol, b, x] = (middle * fgain[:, lanes]).astype(BF)
        for o in (1, 3, 2):
            z_send(b, o).start()
        for d in (1, 3, 2):
            x_send(b, 0, d).start()

    def forward(b, o):
        z_arrival(b, o).wait_recv()
        for d in (1, 3, 2):
            x_send(b, o, d).start()

    def turn(n, carry):
        after = n + 1

        @pl.when((n < 7) & (after % 4 > 0))
        def _():
            q_arrival(after // 4, after % 4, 0).wait_recv()

        @pl.when(n < 7)
        def _():
            q_arrival(after // 4, after % 4, 1).wait_recv()
            q_hand(after // 4, after % 4).start()

        q_handed(n // 4, n % 4).wait_recv()
        attend(n)
        half_send(n).start()

        @pl.when(n == 0)
        def _():
            for t, dy in others:
                q_send(1, t, dy).start()

        @pl.when(n >= 1)
        def _():
            merge(n - 1)

        @pl.when(n == 5)
        def _():
            wo_load.wait()
            project(0)

        for m in range(1, 3):

            @pl.when(n == 2 * m - 2)
            def _():
                w_copy(0, m).start()

        for m in range(3):

            @pl.when(n == 4 + m)
            def _():
                w_copy(0, m).wait_recv()
                w_copy(1, m).wait_recv()
                w_copy(6, m).start()
                w_copy(3, m).start()
                w_copy(4, m).start()

        return carry

    lax.fori_loop(0, 8, turn, 0)
    merge(7)
    residual(0)

    project(1)
    for o in (1, 3, 2):
        forward(0, o)
    residual(1)
    mid_send = remote(mid.at[1 - zpar], midr, ms, mr, tensor=zmate)
    mid_send.start()
    for o in (1, 3, 2):
        forward(1, o)

    for copy in own_loads:
        copy.wait()

    def gate_up(block, first, last):
        lanes = pl.ds(pl.multiple_of(block * 1024, 1024), 1024)
        piece = fbuf[block].reshape(128, 1024)
        units = 80 * (last - first)
        return [
            lax.dot_general(piece, wall[m, first:last, :, lanes].reshape(units, 1024), NT, preferred_element_type=F32)
            for m in range(2)
        ]

    def activate(sums, scale):
        gate = sums[0] * scale
        return (jax.nn.gelu(gate, approximate=True) * (sums[1] * scale)).astype(BF)

    for m in range(2):
        for kind in (2, 3, 4):
            w_copy(kind, m).wait_recv()
    squares = jnp.zeros((128, 1), F32)
    for n, o in enumerate((0, 1, 3, 2)):
        for b in range(2):
            for d in (1, 3, 2):
                x_arrival(b, o, d).wait_recv()
        block = ((z + 8 - 2 * o) % 8) // 2
        plain = fbuf[block].reshape(128, 1024).astype(F32) / fgain[:, pl.ds(pl.multiple_of(block * 1024, 1024), 1024)]
        squares = squares + jnp.sum(plain * plain, axis=-1, keepdims=True)
        for m, product in enumerate(gate_up(block, 0, 6)):
            if n == 0:
                acc[m] = product
            else:
                acc[m] += product
    scale = lax.rsqrt(squares * (1.0 / 4096) + EPS)
    hidden = activate(acc, scale)

    for kind in (2, 3, 4):
        w_copy(kind, 2).wait_recv()
    for k in range(4):
        lanes = pl.ds(pl.multiple_of(((zcol + k) % 4) * 1024, 1024), 1024)
        product = jnp.dot(hidden, wall[2, 0:6, :, lanes].reshape(480, 1024), preferred_element_type=F32)
        for b in range(2):
            oown[k, :, b] = product[64 * b : 64 * (b + 1)].reshape(4, 16, 1024)

    for m in range(3):
        w_copy(6, m).wait_recv()
        w_copy(5, m).start()
    for m in range(2):
        w_copy(5, m).wait_recv()
    late = [jnp.zeros((128, 160), F32), jnp.zeros((128, 160), F32)]
    for block in range(4):
        for m, product in enumerate(gate_up(block, 6, 8)):
            late[m] = late[m] + product
    hidden = activate(late, scale)

    w_copy(5, 2).wait_recv()

    def o_send(block, k, d):
        return remote(osend.at[block, (x + d) % 4], orecv.at[k, d], os_.at[k, d], or_.at[k, d], passage=peer(d, 0))

    for k in (2, 1, 3, 0):
        block = (zcol + k) % 4
        lanes = pl.ds(pl.multiple_of(block * 1024, 1024), 1024)
        product = jnp.dot(hidden, wall[2, 6:8, :, lanes].reshape(160, 1024), preferred_element_type=F32)
        for b in range(2):
            half = oown[k, :, b] + product[64 * b : 64 * (b + 1)].reshape(4, 16, 1024)
            osend[block, :, b] = half.astype(BF)
            oown[k, :, b] = half
        for d in (1, 3, 2):
            o_send(block, k, d).start()

    def f_send(o):
        to = (z + o) % 8
        return remote(fsend.at[to // 2, to % 2], frecv.at[o], fs.at[o], fr.at[o], tensor=to)

    for k in (2, 1, 3, 0):
        block = (zcol + k) % 4
        total = oown[k, x].reshape(32, 1024)
        for d in (1, 3, 2):
            o_send(block, k, d).wait_recv()
            total = total + orecv[k, d].reshape(32, 1024).astype(F32)
        fsend[block, 0] = total[:, :512].astype(BF)
        fsend[block, 1] = total[:, 512:].astype(BF)
        if k == 0:
            fown[0] = total[:, :512]
            fown[1] = total[:, 512:]
            f_send((zmate - z + 8) % 8).start()
        else:
            for e in range(2):
                f_send((2 * block + e - z + 8) % 8).start()

    mid_send.wait_recv()
    mine = mid[zpar] + fown[zpar]
    other = midr[...]
    for o in range(1, 8):
        f_send(o).wait_recv()
        if o % 2 == 0:
            mine = mine + frecv[o].astype(F32)
        else:
            other = other + frecv[o].astype(F32)
    for b in range(2):
        part = slice(16 * b, 16 * (b + 1))
        out_ref[pl.ds(pl.multiple_of(32 * b + zpar * 16, 16), 16), :] = mine[part].astype(BF)
        out_ref[pl.ds(pl.multiple_of(32 * b + 16 - zpar * 16, 16), 16), :] = other[part].astype(BF)

    for b in range(2):
        for t, dy in others:
            q_send(b, t, dy).wait_send()
            part_send(b, t, dy).wait_send()
        for t in range(4):
            q_hand(b, t).wait_send()
            half_send(4 * b + t).wait_send()
        for o in range(1, 8):
            wo_send(b, o).wait_send()
        for o in range(4):
            if o > 0:
                z_send(b, o).wait_send()
            for d in (1, 2, 3):
                x_send(b, o, d).wait_send()
    for m in range(3):
        for kind in range(7):
            w_copy(kind, m).wait_send()
    mid_send.wait_send()
    for o in range(1, 8):
        f_send(o).wait_send()
    for k in range(4):
        for d in (1, 2, 3):
            o_send((zcol + k) % 4, k, d).wait_send()


def on_device(
    answer_states, cross_keys, cross_values, passage_lengths, passage_sources, source_bias,
    query_weight, output_weight, attn_gain, ffn_gain, gate_weight, up_weight, down_weight,
):
    hbm = pl.BlockSpec(memory_space=pl.ANY)
    smem = pl.BlockSpec(memory_space=pltpu.SMEM)
    vmem = pl.BlockSpec(memory_space=pltpu.VMEM)
    dma = pltpu.SemaphoreType.DMA
    return pl.pallas_call(
        block_kernel,
        out_shape=jax.ShapeDtypeStruct((64, 512), BF),
        in_specs=[hbm, hbm, hbm, smem, smem, smem, hbm, hbm, vmem, vmem, hbm, hbm, hbm],
        out_specs=vmem,
        scratch_shapes=[
            pltpu.VMEM((64, 4096), BF),
            pltpu.VMEM((4096, 512), BF),
            pltpu.VMEM((512, 4096), BF),
            pltpu.VMEM((4, 1024, 256), BF),
            pltpu.VMEM((4, 1024, 256), BF),
            pltpu.VMEM((256, 128), BF),
            pltpu.VMEM((1536, 128), BF),
            pltpu.VMEM((128, 512), BF),
            pltpu.VMEM((2, 4, 2, 2, 32, 512), BF),
            pltpu.VMEM((8, 2, 3, 64, 512), F32),
            pltpu.VMEM((8, 3, 64, 512), F32),
            pltpu.VMEM((8, 2, 32, 640), BF),
            pltpu.VMEM((2, 4, 2, 32, 640), BF),
            pltpu.VMEM((2, 4, 2, 16, 1024), BF),
            pltpu.VMEM((2, 8, 16, 1024), BF),
            pltpu.VMEM((2, 2, 16, 1024), F32),
            pltpu.VMEM((2, 32, 512), F32),
            pltpu.VMEM((32, 512), F32),
            pltpu.VMEM((4, 2, 4, 16, 1024), BF),
            pltpu.VMEM((2, 128, 480), F32),
            pltpu.VMEM((4, 4, 2, 16, 1024), F32),
            pltpu.VMEM((4, 4, 2, 16, 1024), BF),
            pltpu.VMEM((4, 4, 2, 16, 1024), BF),
            pltpu.VMEM((2, 32, 512), F32),
            pltpu.VMEM((4, 2, 32, 512), BF),
            pltpu.VMEM((8, 32, 512), BF),
            pltpu.VMEM((3, 8, 80, 4096), BF),
            dma((13,)), dma((4,)),
            dma((7, 3)), dma((7, 3)),
            dma((2, 4, 2)), dma((2, 4, 2)), dma((2, 4)), dma((2, 4)),
            dma((8,)), dma((8,)), dma((2, 4, 2)), dma((2, 4, 2)),
            dma((2, 8)), dma((2, 8)), dma, dma,
            dma((2, 4)), dma((2, 4)), dma((2, 4, 4)), dma((2, 4, 4)),
            dma((4, 4)), dma((4, 4)), dma((8,)), dma((8,)),
        ],
        compiler_params=pltpu.CompilerParams(
            collective_id=0, has_side_effects=True, vmem_limit_bytes=60 * 1024 * 1024
        ),
        cost_estimate=pl.CostEstimate(flops=5_000_000_000, bytes_accessed=14_000_000, transcendentals=9_000_000),
        name="decoder_block",
    )(
        answer_states, cross_keys, cross_values, passage_lengths, passage_sources, source_bias.T,
        query_weight, output_weight, attn_gain.reshape(1, 4096), ffn_gain.reshape(1, 4096),
        gate_weight.T, up_weight.T, down_weight,
    )


def solution(mesh):
    return jax.shard_map(
        on_device,
        mesh=mesh,
        in_specs=(
            P(("dp", "passage"), None),
            P(("dp", "passage"), "tensor"),
            P(("dp", "passage"), "tensor"),
            P(("dp", "passage")),
            P(("dp", "passage")),
            P(None, "tensor"),
            P(None, "tensor"),
            P("tensor", None),
            P(),
            P(),
            P(None, ("tensor", "passage")),
            P(None, ("tensor", "passage")),
            P(("tensor", "passage"), None),
        ),
        out_specs=P(("dp", "passage"), "tensor"),
        check_vma=False,
    )
```

```python
import functools

import jax
import jax.numpy as jnp
from jax import lax
from jax.experimental import pallas as pl
from jax.experimental.pallas import tpu as pltpu
from jax.sharding import PartitionSpec as P

PLEN = 256
EPS = 1e-06
BF = jnp.bfloat16
F32 = jnp.float32
MESH = pl.DeviceIdType.MESH
NT = (((1,), (1,)), ((), ()))


def remote(src, dst, send_sem, recv_sem, **where):
    return pltpu.make_async_remote_copy(
        src_ref=src,
        dst_ref=dst,
        send_sem=send_sem,
        recv_sem=recv_sem,
        device_id=where,
        device_id_type=MESH,
    )


def iota(shape, axis):
    return lax.broadcasted_iota(jnp.int32, shape, axis)


def block_kernel(
    states_h, keys_h, values_h, lens_s, srcs_s, bias_s, wq_h, wo_h, again, fgain, gate_h, up_h, down_h,
    out_ref,
    states, wq, wo, kaug, vaug, qaug, sel, expand,
    qall, ostage, srecv, rsend, rrecv,
    wsend, wrecv, wown, mid, midr, sq, sqin, fbuf, acc, oown, osend, orecv, fown, fsend, frecv, wall,
    load_sem, wq_sem, ws, wr, qs, qr, qfs, qfr, ss, sr, rs, rr, as_, ar, ms, mr,
    zs, zr, xs, xr, os_, or_, fs, fr, sqs, sqr,
):
    dp = lax.axis_index("dp")
    z = lax.axis_index("tensor")
    p = lax.axis_index("passage")
    x = p // 4
    yl = (p // 2) % 2
    c = p % 2
    sib = p + 1 - 2 * c
    zpar = z % 2
    zcol = z // 2
    zmate = z + 1 - 2 * zpar

    def peer(dx, dy):
        return ((x + dx) % 4) * 4 + ((yl + dy) % 2) * 2 + c

    def shift(t):
        return t + t // 2 - 2 * (t // 3)

    ydev = dict(dp=(dp + c) % 2, passage=peer(0, 1))
    yfar = dict(dp=1 - dp, passage=peer(0, 1))
    zdev = dict(tensor=(z + 1 - 2 * c + 8) % 8)

    barrier = pltpu.get_barrier_semaphore()
    for i in range(1, 8):
        pl.semaphore_signal(barrier, inc=1, device_id={"passage": peer(i // 2, i % 2)}, device_id_type=MESH)
        pl.semaphore_signal(barrier, inc=1, device_id={"tensor": (z + i) % 8}, device_id_type=MESH)
    pl.semaphore_signal(barrier, inc=1, device_id={"passage": sib}, device_id_type=MESH)
    pl.semaphore_signal(barrier, inc=1, device_id=yfar, device_id_type=MESH)

    states_load = pltpu.make_async_copy(states_h, states, load_sem.at[0])
    states_load.start()
    wq_loads = []
    for k in range(4):
        rows = pl.ds(1024 * k, 1024)
        wq_loads.append(pltpu.make_async_copy(wq_h.at[rows], wq.at[rows], wq_sem.at[k]))
        wq_loads[k].start()
    kv_loads = []
    for j in range(4):
        lanes = pl.ds(128 * j, 128)
        kv_loads.append(pltpu.make_async_copy(keys_h.at[:, lanes], kaug.at[j, :, pl.ds(0, 128)], load_sem.at[2 + j]))
        kv_loads.append(pltpu.make_async_copy(values_h.at[:, lanes], vaug.at[j, :, pl.ds(0, 128)], load_sem.at[6 + j]))
    wo_load = pltpu.make_async_copy(wo_h, wo, load_sem.at[1])
    own_loads = [
        pltpu.make_async_copy(ref, wall.at[m, 0], load_sem.at[10 + m]) for m, ref in enumerate((gate_h, up_h, down_h))
    ]

    states_load.wait()
    square = jnp.zeros((64, 1), F32)
    for k in range(4):
        part = states[:, 1024 * k : 1024 * (k + 1)].astype(F32)
        square = square + jnp.sum(part * part, axis=-1, keepdims=True)
    scale = lax.rsqrt(square * (1.0 / 4096) + EPS)
    query = jnp.zeros((64, 512), F32)
    for k in range(4):
        cols = slice(1024 * k, 1024 * (k + 1))
        normed = (states[:, cols].astype(F32) * scale * again[:, cols]).astype(BF)
        wq_loads[k].wait()
        query = query + jnp.dot(normed, wq[cols, :], preferred_element_type=F32)
    for copy in kv_loads:
        copy.start()
    qall[0, x, c, yl] = query[:32].astype(BF)
    qall[1, x, c, yl] = query[32:].astype(BF)

    pl.semaphore_wait(barrier, 16)

    def q_send(b, t, dy):
        slot = qall.at[b, x, c, yl]
        return remote(slot, slot, qs.at[b, t, dy], qr.at[b, t, dy], passage=peer(shift(t), dy))

    def q_arrival(b, t, dy):
        slot = qall.at[b, (x + 4 - shift(t)) % 4, c, (yl + dy) % 2]
        return remote(slot, slot, qs.at[b, t, dy], qr.at[b, t, dy], passage=peer(shift(t), dy))

    def q_hand(b, t):
        slab = qall.at[b, (x + 4 - shift(t)) % 4, c]
        return remote(slab, slab, qfs.at[b, t], qfr.at[b, t], passage=sib)

    def q_handed(b, t):
        slab = qall.at[b, (x + 4 - shift(t)) % 4, 1 - c]
        return remote(slab, slab, qfs.at[b, t], qfr.at[b, t], passage=sib)

    others = [(t, dy) for t in range(4) for dy in range(2) if (t, dy) != (0, 0)]
    for t, dy in others:
        q_send(0, t, dy).start()

    def w_copy(kind, m):
        own = (gate_h, up_h, down_h)[m]
        if kind == 0:
            src, slot, dev = own, 2, yfar if m == 2 else ydev
        elif kind == 1:
            src, slot, dev = own, 4, zdev
        elif kind == 2:
            src, slot, dev = own, 1, dict(passage=sib)
        elif kind < 6:
            src, slot, dev = wall.at[m, 2 * kind - 4], 2 * kind - 3, dict(passage=sib)
        else:
            src, slot, dev = wall.at[m, 4], 6, ydev
        return remote(src, wall.at[m, slot], ws.at[kind, m], wr.at[kind, m], **dev)

    w_copy(0, 0).start()
    for m in range(3):
        w_copy(1, m).start()

    lane = iota((256, 128), 1)
    row = iota((256, 128), 0)
    for j in range(4):
        for pp in range(4):
            table = jnp.where(lane == 0, jnp.where(row >= lens_s[pp], F32(-1e30), F32(0)), F32(0))
            for e in range(2):
                value = jnp.full((256, 128), bias_s[2 * j + e, srcs_s[pp]], F32)
                high = value.astype(BF).astype(F32)
                middle = (value - high).astype(BF).astype(F32)
                low = value - high - middle
                first = 1 + 3 * e
                table = jnp.where(lane == first, high, table)
                table = jnp.where(lane == first + 1, middle, table)
                table = jnp.where(lane == first + 2, low, table)
            kaug[j, 256 * pp : 256 * (pp + 1), 128:256] = table.astype(BF)
        vaug[j, :, 128:256] = jnp.ones((1024, 128), BF)
    upper = row < 128
    qaug[...] = jnp.where(
        (lane == 0) | (upper & (lane >= 1) & (lane < 4)) | (~upper & (lane >= 4) & (lane < 7)), F32(1), F32(0)
    ).astype(BF)
    srow, scol = iota((1536, 128), 0), iota((1536, 128), 1)
    sel[...] = jnp.where((srow % 64 == 0) & (scol == srow // 64), F32(1), F32(0)).astype(BF)
    erow, ecol = iota((128, 512), 0), iota((128, 512), 1)
    expand[...] = jnp.where((erow < 24) & (erow % 8 == ecol // 64), F32(1), F32(0)).astype(BF)
    q_arrival(0, 0, 1).wait_recv()
    q_hand(0, 0).start()
    for copy in kv_loads:
        copy.wait()
    wo_load.start()
    for copy in own_loads:
        copy.start()
    for m in range(3):
        w_copy(2, m).start()

    def attend(n):
        rows = qall[n // 4, (x + 4 - shift(n % 4)) % 4].reshape(128, 512)
        head_lane = iota((128, 128), 1) < 64
        zero = jnp.zeros((128, 128), BF)
        for j in range(4):
            cols = slice(128 * j, 128 * (j + 1))
            pair = rows[:, cols]
            both = jnp.concatenate([jnp.where(head_lane, pair, zero), jnp.where(head_lane, zero, pair)], axis=0)
            both = jnp.concatenate([both, qaug[...]], axis=1)
            scores = lax.dot_general(both, kaug[j], NT, preferred_element_type=F32)
            peak = jnp.max(scores, axis=1, keepdims=True)
            weights = jnp.exp(scores - peak).astype(BF)
            result = jnp.dot(weights, vaug[j], preferred_element_type=F32)
            part = jnp.where(head_lane, result[:128, :128], result[128:, :128])
            total = jnp.where(head_lane, result[:128, 128:], result[128:, 128:])
            peak = jnp.where(head_lane, peak[:128], peak[128:])
            for e in range(2):
                half = slice(64 * e, 64 * (e + 1))
                ostage[n, e, 0, :, cols] = part[half]
                ostage[n, e, 1, :, cols] = total[half]
                ostage[n, e, 2, :, cols] = peak[half]

    def half_send(n):
        return remote(ostage.at[n, 1 - c], srecv.at[n], ss.at[n], sr.at[n], passage=sib)

    def part_send(b, t, dy):
        to = ((x + 4 - shift(t)) % 4) * 4 + ((yl + dy) % 2) * 2 + c
        return remote(
            rsend.at[4 * b + t, (yl + dy) % 2], rrecv.at[b, t, dy], rs.at[b, t, dy], rr.at[b, t, dy], passage=to
        )

    def merge(n):
        half_send(n).wait_recv()
        peak_a, peak_b = ostage[n, c, 2], srecv[n, 2]
        highest = jnp.maximum(peak_a, peak_b)
        weight_a = jnp.exp(peak_a - highest)
        weight_b = jnp.exp(peak_b - highest)
        total = weight_a * ostage[n, c, 1] + weight_b * srecv[n, 1]
        part = ((weight_a * ostage[n, c, 0] + weight_b * srecv[n, 0]) / total).astype(BF)
        level = highest + jnp.log(total)
        high = level.astype(BF)
        rest = level - high.astype(F32)
        middle = rest.astype(BF)
        low = (rest - middle.astype(F32)).astype(BF)
        pieces = jnp.concatenate([high, middle, low], axis=1)
        packed = jnp.dot(pieces, sel[...], preferred_element_type=F32).astype(BF)
        for e in range(2):
            rsend[n, e, :, 0:512] = part[32 * e : 32 * (e + 1)]
            rsend[n, e, :, 512:640] = packed[32 * e : 32 * (e + 1)]
        b, t = n // 4, n % 4
        part_send(b, t, 1).start()

        @pl.when(t > 0)
        def _():
            part_send(b, t, 0).start()

    def wo_send(b, o):
        to = (z + o) % 8
        return remote(wsend.at[b, to // 2, to % 2], wrecv.at[b, o], as_.at[b, o], ar.at[b, o], tensor=to)

    def project(b):
        for t, dy in others:
            part_send(b, t, dy).wait_recv()
        parts = [rsend[4 * b, yl]] + [rrecv[b, t, dy] for t, dy in others]
        levels = [jnp.dot(part[:, 512:640], expand[...], preferred_element_type=F32) for part in parts]
        highest = functools.reduce(jnp.maximum, levels)
        total = jnp.zeros((32, 512), F32)
        joined = jnp.zeros((32, 512), F32)
        for part, level in zip(parts, levels):
            weight = jnp.exp(level - highest)
            total = total + weight
            joined = joined + weight * part[:, 0:512].astype(F32)
        attended = (joined / total).astype(BF)
        for k in (2, 1, 3, 0):
            block = (zcol + k) % 4
            lanes = pl.ds(pl.multiple_of(block * 1024, 1024), 1024)
            product = jnp.dot(attended, wo[:, lanes], preferred_element_type=F32)
            wsend[b, block, 0] = product[:16].astype(BF)
            wsend[b, block, 1] = product[16:].astype(BF)
            if k == 0:
                wown[b, 0] = product[:16]
                wown[b, 1] = product[16:]
                wo_send(b, (zmate - z + 8) % 8).start()
            else:
                for e in range(2):
                    wo_send(b, (2 * block + e - z + 8) % 8).start()

    def z_send(b, o):
        slot = fbuf.at[zcol, b, x]
        return remote(slot, slot, zs.at[b, o], zr.at[b, o], tensor=(z + 2 * o) % 8)

    def z_arrival(b, o):
        slot = fbuf.at[((z + 8 - 2 * o) % 8) // 2, b, x]
        return remote(slot, slot, zs.at[b, o], zr.at[b, o], tensor=(z + 2 * o) % 8)

    def x_send(b, o, d):
        slot = fbuf.at[((z + 8 - 2 * o) % 8) // 2, b, x]
        return remote(slot, slot, xs.at[b, o, d], xr.at[b, o, d], passage=peer(d, 0))

    def x_arrival(b, o, d):
        slot = fbuf.at[((z + 8 - 2 * o) % 8) // 2, b, (x + 4 - d) % 4]
        return remote(slot, slot, xs.at[b, o, d], xr.at[b, o, d], passage=peer(d, 0))

    def residual(b):
        lanes = pl.ds(pl.multiple_of(zcol * 1024, 1024), 1024)
        rows = pl.ds(pl.multiple_of(32 * b + zpar * 16, 16), 16)
        middle = states[rows, lanes].astype(F32) + wown[b, zpar]
        for o in range(1, 8):
            wo_send(b, o).wait_recv()
            middle = middle + wrecv[b, o].astype(F32)
        mid[0, 16 * b : 16 * b + 16] = middle[:, :512]
        mid[1, 16 * b : 16 * b + 16] = middle[:, 512:]
        square = jnp.sum(middle * middle, axis=-1, keepdims=True)
        sq[b] = jnp.broadcast_to(square, (16, 128))
        for o in (1, 3, 2):
            sq_send(b, o).start()

    def sq_send(b, o):
        return remote(sq.at[b], sqin.at[b, o], sqs.at[b, o], sqr.at[b, o], tensor=(z + 2 * o) % 8)

    def normalise(b):
        square = sq[b]
        for o in (1, 2, 3):
            sq_send(b, o).wait_recv()
            square = square + sqin[b, o]
        scale = lax.rsqrt(square * (1.0 / 4096) + EPS)[:, :1]
        for e in range(2):
            lanes = pl.ds(pl.multiple_of(zcol * 1024 + 512 * e, 512), 512)
            fbuf[zcol, b, x, :, 512 * e : 512 * (e + 1)] = (
                mid[e, 16 * b : 16 * b + 16] * scale * fgain[:, lanes]
            ).astype(BF)
        for o in (1, 3, 2):
            z_send(b, o).start()
        for d in (1, 3, 2):
            x_send(b, 0, d).start()

    def forward(b, o):
        z_arrival(b, o).wait_recv()
        for d in (1, 3, 2):
            x_send(b, o, d).start()

    def turn(n, carry):
        after = n + 1

        @pl.when((n < 7) & (after % 4 > 0))
        def _():
            q_arrival(after // 4, after % 4, 0).wait_recv()

        @pl.when(n < 7)
        def _():
            q_arrival(after // 4, after % 4, 1).wait_recv()
            q_hand(after // 4, after % 4).start()

        q_handed(n // 4, n % 4).wait_recv()
        attend(n)
        half_send(n).start()

        @pl.when(n == 0)
        def _():
            for t, dy in others:
                q_send(1, t, dy).start()

        @pl.when(n >= 1)
        def _():
            merge(n - 1)

        @pl.when(n == 5)
        def _():
            wo_load.wait()
            project(0)

        for m in range(1, 3):

            @pl.when(n == 2 * m - 2)
            def _():
                w_copy(0, m).start()

        for m in range(3):

            @pl.when(n == 4 + m)
            def _():
                w_copy(0, m).wait_recv()
                w_copy(1, m).wait_recv()
                w_copy(6, m).start()
                w_copy(3, m).start()
                w_copy(4, m).start()

        return carry

    lax.fori_loop(0, 8, turn, 0)
    merge(7)
    residual(0)

    project(1)
    normalise(0)
    for o in (1, 3, 2):
        forward(0, o)
    residual(1)
    normalise(1)
    mid_send = remote(mid.at[1 - zpar], midr, ms, mr, tensor=zmate)
    mid_send.start()
    for o in (1, 3, 2):
        forward(1, o)

    for copy in own_loads:
        copy.wait()

    def gate_up(block, first, last):
        lanes = pl.ds(pl.multiple_of(block * 1024, 1024), 1024)
        piece = fbuf[block].reshape(128, 1024)
        units = 80 * (last - first)
        return [
            lax.dot_general(piece, wall[m, first:last, :, lanes].reshape(units, 1024), NT, preferred_element_type=F32)
            for m in range(2)
        ]

    def activate(sums):
        return (jax.nn.gelu(sums[0], approximate=True) * sums[1]).astype(BF)

    for m in range(2):
        for kind in (2, 3, 4):
            w_copy(kind, m).wait_recv()
    for n, o in enumerate((0, 1, 3, 2)):
        for b in range(2):
            for d in (1, 3, 2):
                x_arrival(b, o, d).wait_recv()
        block = ((z + 8 - 2 * o) % 8) // 2
        for m, product in enumerate(gate_up(block, 0, 6)):
            if n == 0:
                acc[m] = product
            else:
                acc[m] += product
    hidden = activate(acc)

    for kind in (2, 3, 4):
        w_copy(kind, 2).wait_recv()
    for k in range(4):
        lanes = pl.ds(pl.multiple_of(((zcol + k) % 4) * 1024, 1024), 1024)
        product = jnp.dot(hidden, wall[2, 0:6, :, lanes].reshape(480, 1024), preferred_element_type=F32)
        for b in range(2):
            oown[k, :, b] = product[64 * b : 64 * (b + 1)].reshape(4, 16, 1024)

    for m in range(3):
        w_copy(6, m).wait_recv()
        w_copy(5, m).start()
    for m in range(2):
        w_copy(5, m).wait_recv()
    late = [jnp.zeros((128, 160), F32), jnp.zeros((128, 160), F32)]
    for block in range(4):
        for m, product in enumerate(gate_up(block, 6, 8)):
            late[m] = late[m] + product
    hidden = activate(late)

    w_copy(5, 2).wait_recv()

    def o_send(block, k, d):
        return remote(osend.at[block, (x + d) % 4], orecv.at[k, d], os_.at[k, d], or_.at[k, d], passage=peer(d, 0))

    for k in (2, 1, 3, 0):
        block = (zcol + k) % 4
        lanes = pl.ds(pl.multiple_of(block * 1024, 1024), 1024)
        product = jnp.dot(hidden, wall[2, 6:8, :, lanes].reshape(160, 1024), preferred_element_type=F32)
        for b in range(2):
            half = oown[k, :, b] + product[64 * b : 64 * (b + 1)].reshape(4, 16, 1024)
            osend[block, :, b] = half.astype(BF)
            oown[k, :, b] = half
        for d in (1, 3, 2):
            o_send(block, k, d).start()

    def f_send(o):
        to = (z + o) % 8
        return remote(fsend.at[to // 2, to % 2], frecv.at[o], fs.at[o], fr.at[o], tensor=to)

    for k in (2, 1, 3, 0):
        block = (zcol + k) % 4
        total = oown[k, x].reshape(32, 1024)
        for d in (1, 3, 2):
            o_send(block, k, d).wait_recv()
            total = total + orecv[k, d].reshape(32, 1024).astype(F32)
        fsend[block, 0] = total[:, :512].astype(BF)
        fsend[block, 1] = total[:, 512:].astype(BF)
        if k == 0:
            fown[0] = total[:, :512]
            fown[1] = total[:, 512:]
            f_send((zmate - z + 8) % 8).start()
        else:
            for e in range(2):
                f_send((2 * block + e - z + 8) % 8).start()

    mid_send.wait_recv()
    mine = mid[zpar] + fown[zpar]
    other = midr[...]
    for o in range(1, 8):
        f_send(o).wait_recv()
        if o % 2 == 0:
            mine = mine + frecv[o].astype(F32)
        else:
            other = other + frecv[o].astype(F32)
    for b in range(2):
        part = slice(16 * b, 16 * (b + 1))
        out_ref[pl.ds(pl.multiple_of(32 * b + zpar * 16, 16), 16), :] = mine[part].astype(BF)
        out_ref[pl.ds(pl.multiple_of(32 * b + 16 - zpar * 16, 16), 16), :] = other[part].astype(BF)

    for b in range(2):
        for t, dy in others:
            q_send(b, t, dy).wait_send()
            part_send(b, t, dy).wait_send()
        for t in range(4):
            q_hand(b, t).wait_send()
            half_send(4 * b + t).wait_send()
        for o in range(1, 8):
            wo_send(b, o).wait_send()
        for o in range(4):
            if o > 0:
                sq_send(b, o).wait_send()
                z_send(b, o).wait_send()
            for d in (1, 2, 3):
                x_send(b, o, d).wait_send()
    for m in range(3):
        for kind in range(7):
            w_copy(kind, m).wait_send()
    mid_send.wait_send()
    for o in range(1, 8):
        f_send(o).wait_send()
    for k in range(4):
        for d in (1, 2, 3):
            o_send((zcol + k) % 4, k, d).wait_send()


def on_device(
    answer_states, cross_keys, cross_values, passage_lengths, passage_sources, source_bias,
    query_weight, output_weight, attn_gain, ffn_gain, gate_weight, up_weight, down_weight,
):
    hbm = pl.BlockSpec(memory_space=pl.ANY)
    smem = pl.BlockSpec(memory_space=pltpu.SMEM)
    vmem = pl.BlockSpec(memory_space=pltpu.VMEM)
    dma = pltpu.SemaphoreType.DMA
    return pl.pallas_call(
        block_kernel,
        out_shape=jax.ShapeDtypeStruct((64, 512), BF),
        in_specs=[hbm, hbm, hbm, smem, smem, smem, hbm, hbm, vmem, vmem, hbm, hbm, hbm],
        out_specs=vmem,
        scratch_shapes=[
            pltpu.VMEM((64, 4096), BF),
            pltpu.VMEM((4096, 512), BF),
            pltpu.VMEM((512, 4096), BF),
            pltpu.VMEM((4, 1024, 256), BF),
            pltpu.VMEM((4, 1024, 256), BF),
            pltpu.VMEM((256, 128), BF),
            pltpu.VMEM((1536, 128), BF),
            pltpu.VMEM((128, 512), BF),
            pltpu.VMEM((2, 4, 2, 2, 32, 512), BF),
            pltpu.VMEM((8, 2, 3, 64, 512), F32),
            pltpu.VMEM((8, 3, 64, 512), F32),
            pltpu.VMEM((8, 2, 32, 640), BF),
            pltpu.VMEM((2, 4, 2, 32, 640), BF),
            pltpu.VMEM((2, 4, 2, 16, 1024), BF),
            pltpu.VMEM((2, 8, 16, 1024), BF),
            pltpu.VMEM((2, 2, 16, 1024), F32),
            pltpu.VMEM((2, 32, 512), F32),
            pltpu.VMEM((32, 512), F32),
            pltpu.VMEM((2, 16, 128), F32),
            pltpu.VMEM((2, 4, 16, 128), F32),
            pltpu.VMEM((4, 2, 4, 16, 1024), BF),
            pltpu.VMEM((2, 128, 480), F32),
            pltpu.VMEM((4, 4, 2, 16, 1024), F32),
            pltpu.VMEM((4, 4, 2, 16, 1024), BF),
            pltpu.VMEM((4, 4, 2, 16, 1024), BF),
            pltpu.VMEM((2, 32, 512), F32),
            pltpu.VMEM((4, 2, 32, 512), BF),
            pltpu.VMEM((8, 32, 512), BF),
            pltpu.VMEM((3, 8, 80, 4096), BF),
            dma((13,)), dma((4,)),
            dma((7, 3)), dma((7, 3)),
            dma((2, 4, 2)), dma((2, 4, 2)), dma((2, 4)), dma((2, 4)),
            dma((8,)), dma((8,)), dma((2, 4, 2)), dma((2, 4, 2)),
            dma((2, 8)), dma((2, 8)), dma, dma,
            dma((2, 4)), dma((2, 4)), dma((2, 4, 4)), dma((2, 4, 4)),
            dma((4, 4)), dma((4, 4)), dma((8,)), dma((8,)), dma((2, 4)), dma((2, 4)),
        ],
        compiler_params=pltpu.CompilerParams(
            collective_id=0, has_side_effects=True, vmem_limit_bytes=60 * 1024 * 1024
        ),
        cost_estimate=pl.CostEstimate(flops=5_000_000_000, bytes_accessed=14_000_000, transcendentals=9_000_000),
        name="decoder_block",
    )(
        answer_states, cross_keys, cross_values, passage_lengths, passage_sources, source_bias.T,
        query_weight, output_weight, attn_gain.reshape(1, 4096), ffn_gain.reshape(1, 4096),
        gate_weight.T, up_weight.T, down_weight,
    )


def solution(mesh):
    return jax.shard_map(
        on_device,
        mesh=mesh,
        in_specs=(
            P(("dp", "passage"), None),
            P(("dp", "passage"), "tensor"),
            P(("dp", "passage"), "tensor"),
            P(("dp", "passage")),
            P(("dp", "passage")),
            P(None, "tensor"),
            P(None, "tensor"),
            P("tensor", None),
            P(),
            P(),
            P(None, ("tensor", "passage")),
            P(None, ("tensor", "passage")),
            P(("tensor", "passage"), None),
        ),
        out_specs=P(("dp", "passage"), "tensor"),
        check_vma=False,
    )
```

```python
import functools

import jax
import jax.numpy as jnp
from jax import lax
from jax.experimental import pallas as pl
from jax.experimental.pallas import tpu as pltpu
from jax.sharding import PartitionSpec as P

PLEN = 256
EPS = 1e-06
BF = jnp.bfloat16
F32 = jnp.float32
MESH = pl.DeviceIdType.MESH
NT = (((1,), (1,)), ((), ()))


def remote(src, dst, send_sem, recv_sem, **where):
    return pltpu.make_async_remote_copy(
        src_ref=src,
        dst_ref=dst,
        send_sem=send_sem,
        recv_sem=recv_sem,
        device_id=where,
        device_id_type=MESH,
    )


def iota(shape, axis):
    return lax.broadcasted_iota(jnp.int32, shape, axis)


def block_kernel(
    states_h, keys_h, values_h, lens_s, srcs_s, bias_s, wq_h, wo_h, again, fgain, gate_h, up_h, down_h,
    out_ref,
    states, wq, wo, kaug, vaug, qaug, sel, expand,
    qall, ostage, srecv, rsend, rrecv,
    wsend, wrecv, wown, mid, midr, fbuf, acc, oown, osend, orecv, fown, fsend, frecv, wall,
    load_sem, wq_sem, ws, wr, qs, qr, qfs, qfr, ss, sr, rs, rr, as_, ar, ms, mr,
    zs, zr, xs, xr, os_, or_, fs, fr,
):
    dp = lax.axis_index("dp")
    z = lax.axis_index("tensor")
    p = lax.axis_index("passage")
    x = p // 4
    yl = (p // 2) % 2
    c = p % 2
    sib = p + 1 - 2 * c
    zpar = z % 2
    zcol = z // 2
    zmate = z + 1 - 2 * zpar

    def peer(dx, dy):
        return ((x + dx) % 4) * 4 + ((yl + dy) % 2) * 2 + c

    def shift(t):
        return t + t // 2 - 2 * (t // 3)

    ydev = dict(dp=(dp + c) % 2, passage=peer(0, 1))
    yfar = dict(dp=1 - dp, passage=peer(0, 1))
    zdev = dict(tensor=(z + 1 - 2 * c + 8) % 8)

    barrier = pltpu.get_barrier_semaphore()
    for i in range(1, 8):
        pl.semaphore_signal(barrier, inc=1, device_id={"passage": peer(i // 2, i % 2)}, device_id_type=MESH)
        pl.semaphore_signal(barrier, inc=1, device_id={"tensor": (z + i) % 8}, device_id_type=MESH)
    pl.semaphore_signal(barrier, inc=1, device_id={"passage": sib}, device_id_type=MESH)
    pl.semaphore_signal(barrier, inc=1, device_id=yfar, device_id_type=MESH)

    states_load = pltpu.make_async_copy(states_h, states, load_sem.at[0])
    states_load.start()
    wq_loads = []
    for k in range(4):
        rows = pl.ds(1024 * k, 1024)
        wq_loads.append(pltpu.make_async_copy(wq_h.at[rows], wq.at[rows], wq_sem.at[k]))
        wq_loads[k].start()
    kv_loads = []
    for j in range(4):
        lanes = pl.ds(128 * j, 128)
        kv_loads.append(pltpu.make_async_copy(keys_h.at[:, lanes], kaug.at[j, :, pl.ds(0, 128)], load_sem.at[2 + j]))
        kv_loads.append(pltpu.make_async_copy(values_h.at[:, lanes], vaug.at[j, :, pl.ds(0, 128)], load_sem.at[6 + j]))
    wo_load = pltpu.make_async_copy(wo_h, wo, load_sem.at[1])
    own_loads = [
        pltpu.make_async_copy(ref, wall.at[m, 0], load_sem.at[10 + m]) for m, ref in enumerate((gate_h, up_h, down_h))
    ]

    states_load.wait()
    square = jnp.zeros((64, 1), F32)
    for k in range(4):
        part = states[:, 1024 * k : 1024 * (k + 1)].astype(F32)
        square = square + jnp.sum(part * part, axis=-1, keepdims=True)
    scale = lax.rsqrt(square * (1.0 / 4096) + EPS)
    query = jnp.zeros((64, 512), F32)
    for k in range(4):
        cols = slice(1024 * k, 1024 * (k + 1))
        normed = (states[:, cols].astype(F32) * scale * again[:, cols]).astype(BF)
        wq_loads[k].wait()
        query = query + jnp.dot(normed, wq[cols, :], preferred_element_type=F32)
    for copy in kv_loads:
        copy.start()
    qall[0, x, c, yl] = query[:32].astype(BF)
    qall[1, x, c, yl] = query[32:].astype(BF)

    pl.semaphore_wait(barrier, 16)

    def q_send(b, t, dy):
        slot = qall.at[b, x, c, yl]
        return remote(slot, slot, qs.at[b, t, dy], qr.at[b, t, dy], passage=peer(shift(t), dy))

    def q_arrival(b, t, dy):
        slot = qall.at[b, (x + 4 - shift(t)) % 4, c, (yl + dy) % 2]
        return remote(slot, slot, qs.at[b, t, dy], qr.at[b, t, dy], passage=peer(shift(t), dy))

    def q_hand(b, t):
        slab = qall.at[b, (x + 4 - shift(t)) % 4, c]
        return remote(slab, slab, qfs.at[b, t], qfr.at[b, t], passage=sib)

    def q_handed(b, t):
        slab = qall.at[b, (x + 4 - shift(t)) % 4, 1 - c]
        return remote(slab, slab, qfs.at[b, t], qfr.at[b, t], passage=sib)

    others = [(t, dy) for t in range(4) for dy in range(2) if (t, dy) != (0, 0)]
    for t, dy in others:
        q_send(0, t, dy).start()

    def w_copy(kind, m):
        own = (gate_h, up_h, down_h)[m]
        if kind == 0:
            src, slot, dev = own, 2, yfar if m == 2 else ydev
        elif kind == 1:
            src, slot, dev = own, 4, zdev
        elif kind == 2:
            src, slot, dev = own, 1, dict(passage=sib)
        elif kind < 6:
            src, slot, dev = wall.at[m, 2 * kind - 4], 2 * kind - 3, dict(passage=sib)
        else:
            src, slot, dev = wall.at[m, 4], 6, ydev
        return remote(src, wall.at[m, slot], ws.at[kind, m], wr.at[kind, m], **dev)

    w_copy(0, 0).start()
    for m in range(3):
        w_copy(1, m).start()

    lane = iota((256, 128), 1)
    row = iota((256, 128), 0)
    for j in range(4):
        for pp in range(4):
            table = jnp.where(lane == 0, jnp.where(row >= lens_s[pp], F32(-1e30), F32(0)), F32(0))
            for e in range(2):
                value = jnp.full((256, 128), bias_s[2 * j + e, srcs_s[pp]], F32)
                high = value.astype(BF).astype(F32)
                middle = (value - high).astype(BF).astype(F32)
                low = value - high - middle
                first = 1 + 3 * e
                table = jnp.where(lane == first, high, table)
                table = jnp.where(lane == first + 1, middle, table)
                table = jnp.where(lane == first + 2, low, table)
            kaug[j, 256 * pp : 256 * (pp + 1), 128:256] = table.astype(BF)
        vaug[j, :, 128:256] = jnp.ones((1024, 128), BF)
    upper = row < 128
    qaug[...] = jnp.where(
        (lane == 0) | (upper & (lane >= 1) & (lane < 4)) | (~upper & (lane >= 4) & (lane < 7)), F32(1), F32(0)
    ).astype(BF)
    srow, scol = iota((1536, 128), 0), iota((1536, 128), 1)
    sel[...] = jnp.where((srow % 64 == 0) & (scol == srow // 64), F32(1), F32(0)).astype(BF)
    erow, ecol = iota((128, 512), 0), iota((128, 512), 1)
    expand[...] = jnp.where((erow < 24) & (erow % 8 == ecol // 64), F32(1), F32(0)).astype(BF)
    q_arrival(0, 0, 1).wait_recv()
    q_hand(0, 0).start()
    for copy in kv_loads:
        copy.wait()
    wo_load.start()
    for copy in own_loads:
        copy.start()
    for m in range(3):
        w_copy(2, m).start()

    def attend(n):
        rows = qall[n // 4, (x + 4 - shift(n % 4)) % 4].reshape(128, 512)
        head_lane = iota((128, 128), 1) < 64
        zero = jnp.zeros((128, 128), BF)

        def score(j):
            pair = rows[:, 128 * j : 128 * (j + 1)]
            both = jnp.concatenate([jnp.where(head_lane, pair, zero), jnp.where(head_lane, zero, pair)], axis=0)
            both = jnp.concatenate([both, qaug[...]], axis=1)
            return lax.dot_general(both, kaug[j], NT, preferred_element_type=F32)

        following = score(0)
        for j in range(4):
            cols = slice(128 * j, 128 * (j + 1))
            scores = following
            if j < 3:
                following = score(j + 1)
            peak = jnp.max(scores, axis=1, keepdims=True)
            weights = jnp.exp(scores - peak).astype(BF)
            result = jnp.dot(weights, vaug[j], preferred_element_type=F32)
            part = jnp.where(head_lane, result[:128, :128], result[128:, :128])
            total = jnp.where(head_lane, result[:128, 128:], result[128:, 128:])
            peak = jnp.where(head_lane, peak[:128], peak[128:])
            for e in range(2):
                half = slice(64 * e, 64 * (e + 1))
                ostage[n, e, 0, :, cols] = part[half]
                ostage[n, e, 1, :, cols] = total[half]
                ostage[n, e, 2, :, cols] = peak[half]

    def half_send(n):
        return remote(ostage.at[n, 1 - c], srecv.at[n], ss.at[n], sr.at[n], passage=sib)

    def part_send(b, t, dy):
        to = ((x + 4 - shift(t)) % 4) * 4 + ((yl + dy) % 2) * 2 + c
        return remote(
            rsend.at[4 * b + t, (yl + dy) % 2], rrecv.at[b, t, dy], rs.at[b, t, dy], rr.at[b, t, dy], passage=to
        )

    def merge(n):
        half_send(n).wait_recv()
        peak_a, peak_b = ostage[n, c, 2], srecv[n, 2]
        highest = jnp.maximum(peak_a, peak_b)
        weight_a = jnp.exp(peak_a - highest)
        weight_b = jnp.exp(peak_b - highest)
        total = weight_a * ostage[n, c, 1] + weight_b * srecv[n, 1]
        part = ((weight_a * ostage[n, c, 0] + weight_b * srecv[n, 0]) / total).astype(BF)
        level = highest + jnp.log(total)
        high = level.astype(BF)
        rest = level - high.astype(F32)
        middle = rest.astype(BF)
        low = (rest - middle.astype(F32)).astype(BF)
        pieces = jnp.concatenate([high, middle, low], axis=1)
        packed = jnp.dot(pieces, sel[...], preferred_element_type=F32).astype(BF)
        for e in range(2):
            rsend[n, e, :, 0:512] = part[32 * e : 32 * (e + 1)]
            rsend[n, e, :, 512:640] = packed[32 * e : 32 * (e + 1)]
        b, t = n // 4, n % 4
        part_send(b, t, 1).start()

        @pl.when(t > 0)
        def _():
            part_send(b, t, 0).start()

    def wo_send(b, o):
        to = (z + o) % 8
        return remote(wsend.at[b, to // 2, to % 2], wrecv.at[b, o], as_.at[b, o], ar.at[b, o], tensor=to)

    def project(b):
        for t, dy in others:
            part_send(b, t, dy).wait_recv()
        parts = [rsend[4 * b, yl]] + [rrecv[b, t, dy] for t, dy in others]
        levels = [jnp.dot(part[:, 512:640], expand[...], preferred_element_type=F32) for part in parts]
        highest = functools.reduce(jnp.maximum, levels)
        total = jnp.zeros((32, 512), F32)
        joined = jnp.zeros((32, 512), F32)
        for part, level in zip(parts, levels):
            weight = jnp.exp(level - highest)
            total = total + weight
            joined = joined + weight * part[:, 0:512].astype(F32)
        attended = (joined / total).astype(BF)
        for k in (2, 1, 3, 0):
            block = (zcol + k) % 4
            lanes = pl.ds(pl.multiple_of(block * 1024, 1024), 1024)
            product = jnp.dot(attended, wo[:, lanes], preferred_element_type=F32)
            wsend[b, block, 0] = product[:16].astype(BF)
            wsend[b, block, 1] = product[16:].astype(BF)
            if k == 0:
                wown[b, 0] = product[:16]
                wown[b, 1] = product[16:]
                wo_send(b, (zmate - z + 8) % 8).start()
            else:
                for e in range(2):
                    wo_send(b, (2 * block + e - z + 8) % 8).start()

    def z_send(b, o):
        slot = fbuf.at[zcol, b, x]
        return remote(slot, slot, zs.at[b, o], zr.at[b, o], tensor=(z + 2 * o) % 8)

    def z_arrival(b, o):
        slot = fbuf.at[((z + 8 - 2 * o) % 8) // 2, b, x]
        return remote(slot, slot, zs.at[b, o], zr.at[b, o], tensor=(z + 2 * o) % 8)

    def x_send(b, o, d):
        slot = fbuf.at[((z + 8 - 2 * o) % 8) // 2, b, x]
        return remote(slot, slot, xs.at[b, o, d], xr.at[b, o, d], passage=peer(d, 0))

    def x_arrival(b, o, d):
        slot = fbuf.at[((z + 8 - 2 * o) % 8) // 2, b, (x + 4 - d) % 4]
        return remote(slot, slot, xs.at[b, o, d], xr.at[b, o, d], passage=peer(d, 0))

    def residual(b):
        lanes = pl.ds(pl.multiple_of(zcol * 1024, 1024), 1024)
        rows = pl.ds(pl.multiple_of(32 * b + zpar * 16, 16), 16)
        middle = states[rows, lanes].astype(F32) + wown[b, zpar]
        for o in range(1, 8):
            wo_send(b, o).wait_recv()
            middle = middle + wrecv[b, o].astype(F32)
        mid[0, 16 * b : 16 * b + 16] = middle[:, :512]
        mid[1, 16 * b : 16 * b + 16] = middle[:, 512:]
        fbuf[zcol, b, x] = (middle * fgain[:, lanes]).astype(BF)
        for o in (1, 3, 2):
            z_send(b, o).start()
        for d in (1, 3, 2):
            x_send(b, 0, d).start()

    def forward(b, o):
        z_arrival(b, o).wait_recv()
        for d in (1, 3, 2):
            x_send(b, o, d).start()

    def turn(n, carry):
        after = n + 1

        @pl.when((n < 7) & (after % 4 > 0))
        def _():
            q_arrival(after // 4, after % 4, 0).wait_recv()

        @pl.when(n < 7)
        def _():
            q_arrival(after // 4, after % 4, 1).wait_recv()
            q_hand(after // 4, after % 4).start()

        q_handed(n // 4, n % 4).wait_recv()
        attend(n)
        half_send(n).start()

        @pl.when(n == 0)
        def _():
            for t, dy in others:
                q_send(1, t, dy).start()

        @pl.when(n >= 1)
        def _():
            merge(n - 1)

        @pl.when(n == 5)
        def _():
            wo_load.wait()
            project(0)

        for m in range(1, 3):

            @pl.when(n == 2 * m - 2)
            def _():
                w_copy(0, m).start()

        for m in range(3):

            @pl.when(n == 4 + m)
            def _():
                w_copy(0, m).wait_recv()
                w_copy(1, m).wait_recv()
                w_copy(6, m).start()
                w_copy(3, m).start()
                w_copy(4, m).start()

        return carry

    lax.fori_loop(0, 8, turn, 0)
    merge(7)
    residual(0)

    project(1)
    for o in (1, 3, 2):
        forward(0, o)
    residual(1)
    mid_send = remote(mid.at[1 - zpar], midr, ms, mr, tensor=zmate)
    mid_send.start()
    for o in (1, 3, 2):
        forward(1, o)

    for copy in own_loads:
        copy.wait()

    def gate_up(block, first, last):
        lanes = pl.ds(pl.multiple_of(block * 1024, 1024), 1024)
        piece = fbuf[block].reshape(128, 1024)
        units = 80 * (last - first)
        return [
            lax.dot_general(piece, wall[m, first:last, :, lanes].reshape(units, 1024), NT, preferred_element_type=F32)
            for m in range(2)
        ]

    def activate(sums, scale):
        gate = sums[0] * scale
        return (jax.nn.gelu(gate, approximate=True) * (sums[1] * scale)).astype(BF)

    for m in range(2):
        for kind in (2, 3, 4):
            w_copy(kind, m).wait_recv()
    squares = jnp.zeros((128, 1), F32)
    for n, o in enumerate((0, 1, 3, 2)):
        for b in range(2):
            for d in (1, 3, 2):
                x_arrival(b, o, d).wait_recv()
        block = ((z + 8 - 2 * o) % 8) // 2
        plain = fbuf[block].reshape(128, 1024).astype(F32) / fgain[:, pl.ds(pl.multiple_of(block * 1024, 1024), 1024)]
        squares = squares + jnp.sum(plain * plain, axis=-1, keepdims=True)
        for m, product in enumerate(gate_up(block, 0, 6)):
            if n == 0:
                acc[m] = product
            else:
                acc[m] += product
    scale = lax.rsqrt(squares * (1.0 / 4096) + EPS)
    hidden = activate(acc, scale)

    for kind in (2, 3, 4):
        w_copy(kind, 2).wait_recv()
    for k in range(4):
        lanes = pl.ds(pl.multiple_of(((zcol + k) % 4) * 1024, 1024), 1024)
        product = jnp.dot(hidden, wall[2, 0:6, :, lanes].reshape(480, 1024), preferred_element_type=F32)
        for b in range(2):
            oown[k, :, b] = product[64 * b : 64 * (b + 1)].reshape(4, 16, 1024)

    for m in range(3):
        w_copy(6, m).wait_recv()
        w_copy(5, m).start()
    for m in range(2):
        w_copy(5, m).wait_recv()
    late = [jnp.zeros((128, 160), F32), jnp.zeros((128, 160), F32)]
    for block in range(4):
        for m, product in enumerate(gate_up(block, 6, 8)):
            late[m] = late[m] + product
    hidden = activate(late, scale)

    w_copy(5, 2).wait_recv()

    def o_send(block, k, d):
        return remote(osend.at[block, (x + d) % 4], orecv.at[k, d], os_.at[k, d], or_.at[k, d], passage=peer(d, 0))

    for k in (2, 1, 3, 0):
        block = (zcol + k) % 4
        lanes = pl.ds(pl.multiple_of(block * 1024, 1024), 1024)
        product = jnp.dot(hidden, wall[2, 6:8, :, lanes].reshape(160, 1024), preferred_element_type=F32)
        for b in range(2):
            half = oown[k, :, b] + product[64 * b : 64 * (b + 1)].reshape(4, 16, 1024)
            osend[block, :, b] = half.astype(BF)
            oown[k, :, b] = half
        for d in (1, 3, 2):
            o_send(block, k, d).start()

    def f_send(o):
        to = (z + o) % 8
        return remote(fsend.at[to // 2, to % 2], frecv.at[o], fs.at[o], fr.at[o], tensor=to)

    for k in (2, 1, 3, 0):
        block = (zcol + k) % 4
        total = oown[k, x].reshape(32, 1024)
        for d in (1, 3, 2):
            o_send(block, k, d).wait_recv()
            total = total + orecv[k, d].reshape(32, 1024).astype(F32)
        fsend[block, 0] = total[:, :512].astype(BF)
        fsend[block, 1] = total[:, 512:].astype(BF)
        if k == 0:
            fown[0] = total[:, :512]
            fown[1] = total[:, 512:]
            f_send((zmate - z + 8) % 8).start()
        else:
            for e in range(2):
                f_send((2 * block + e - z + 8) % 8).start()

    mid_send.wait_recv()
    mine = mid[zpar] + fown[zpar]
    other = midr[...]
    for o in range(1, 8):
        f_send(o).wait_recv()
        if o % 2 == 0:
            mine = mine + frecv[o].astype(F32)
        else:
            other = other + frecv[o].astype(F32)
    for b in range(2):
        part = slice(16 * b, 16 * (b + 1))
        out_ref[pl.ds(pl.multiple_of(32 * b + zpar * 16, 16), 16), :] = mine[part].astype(BF)
        out_ref[pl.ds(pl.multiple_of(32 * b + 16 - zpar * 16, 16), 16), :] = other[part].astype(BF)

    for b in range(2):
        for t, dy in others:
            q_send(b, t, dy).wait_send()
            part_send(b, t, dy).wait_send()
        for t in range(4):
            q_hand(b, t).wait_send()
            half_send(4 * b + t).wait_send()
        for o in range(1, 8):
            wo_send(b, o).wait_send()
        for o in range(4):
            if o > 0:
                z_send(b, o).wait_send()
            for d in (1, 2, 3):
                x_send(b, o, d).wait_send()
    for m in range(3):
        for kind in range(7):
            w_copy(kind, m).wait_send()
    mid_send.wait_send()
    for o in range(1, 8):
        f_send(o).wait_send()
    for k in range(4):
        for d in (1, 2, 3):
            o_send((zcol + k) % 4, k, d).wait_send()


def on_device(
    answer_states, cross_keys, cross_values, passage_lengths, passage_sources, source_bias,
    query_weight, output_weight, attn_gain, ffn_gain, gate_weight, up_weight, down_weight,
):
    hbm = pl.BlockSpec(memory_space=pl.ANY)
    smem = pl.BlockSpec(memory_space=pltpu.SMEM)
    vmem = pl.BlockSpec(memory_space=pltpu.VMEM)
    dma = pltpu.SemaphoreType.DMA
    return pl.pallas_call(
        block_kernel,
        out_shape=jax.ShapeDtypeStruct((64, 512), BF),
        in_specs=[hbm, hbm, hbm, smem, smem, smem, hbm, hbm, vmem, vmem, hbm, hbm, hbm],
        out_specs=vmem,
        scratch_shapes=[
            pltpu.VMEM((64, 4096), BF),
            pltpu.VMEM((4096, 512), BF),
            pltpu.VMEM((512, 4096), BF),
            pltpu.VMEM((4, 1024, 256), BF),
            pltpu.VMEM((4, 1024, 256), BF),
            pltpu.VMEM((256, 128), BF),
            pltpu.VMEM((1536, 128), BF),
            pltpu.VMEM((128, 512), BF),
            pltpu.VMEM((2, 4, 2, 2, 32, 512), BF),
            pltpu.VMEM((8, 2, 3, 64, 512), F32),
            pltpu.VMEM((8, 3, 64, 512), F32),
            pltpu.VMEM((8, 2, 32, 640), BF),
            pltpu.VMEM((2, 4, 2, 32, 640), BF),
            pltpu.VMEM((2, 4, 2, 16, 1024), BF),
            pltpu.VMEM((2, 8, 16, 1024), BF),
            pltpu.VMEM((2, 2, 16, 1024), F32),
            pltpu.VMEM((2, 32, 512), F32),
            pltpu.VMEM((32, 512), F32),
            pltpu.VMEM((4, 2, 4, 16, 1024), BF),
            pltpu.VMEM((2, 128, 480), F32),
            pltpu.VMEM((4, 4, 2, 16, 1024), F32),
            pltpu.VMEM((4, 4, 2, 16, 1024), BF),
            pltpu.VMEM((4, 4, 2, 16, 1024), BF),
            pltpu.VMEM((2, 32, 512), F32),
            pltpu.VMEM((4, 2, 32, 512), BF),
            pltpu.VMEM((8, 32, 512), BF),
            pltpu.VMEM((3, 8, 80, 4096), BF),
            dma((13,)), dma((4,)),
            dma((7, 3)), dma((7, 3)),
            dma((2, 4, 2)), dma((2, 4, 2)), dma((2, 4)), dma((2, 4)),
            dma((8,)), dma((8,)), dma((2, 4, 2)), dma((2, 4, 2)),
            dma((2, 8)), dma((2, 8)), dma, dma,
            dma((2, 4)), dma((2, 4)), dma((2, 4, 4)), dma((2, 4, 4)),
            dma((4, 4)), dma((4, 4)), dma((8,)), dma((8,)),
        ],
        compiler_params=pltpu.CompilerParams(
            collective_id=0, has_side_effects=True, vmem_limit_bytes=60 * 1024 * 1024
        ),
        cost_estimate=pl.CostEstimate(flops=5_000_000_000, bytes_accessed=14_000_000, transcendentals=9_000_000),
        name="decoder_block",
    )(
        answer_states, cross_keys, cross_values, passage_lengths, passage_sources, source_bias.T,
        query_weight, output_weight, attn_gain.reshape(1, 4096), ffn_gain.reshape(1, 4096),
        gate_weight.T, up_weight.T, down_weight,
    )


def solution(mesh):
    return jax.shard_map(
        on_device,
        mesh=mesh,
        in_specs=(
            P(("dp", "passage"), None),
            P(("dp", "passage"), "tensor"),
            P(("dp", "passage"), "tensor"),
            P(("dp", "passage")),
            P(("dp", "passage")),
            P(None, "tensor"),
            P(None, "tensor"),
            P("tensor", None),
            P(),
            P(),
            P(None, ("tensor", "passage")),
            P(None, ("tensor", "passage")),
            P(("tensor", "passage"), None),
        ),
        out_specs=P(("dp", "passage"), "tensor"),
        check_vma=False,
    )
```
